512 devices in a mesh: ctx: 32 (over x, z_hi, core), resp: 16 (over z_lo, y).
Axes of the slice: x: 4, y: 4, z: 16 (z_hi: 4, z_lo: 4; z = z_hi * 4 + z_lo), core: 2. Of those that a mesh axis runs over, the one named last changes fastest.
Arguments:
- queries: bfloat16 [16, 4096, 4096], P('resp', 'ctx'), may hold values from -96 to 96
- attention_output: bfloat16 [16, 4096, 4096], P('resp', 'ctx'), may hold values from -6 to 6
- grad_out: bfloat16 [16, 4096, 4096], P('resp', 'ctx'), may hold values from -6 to 6
- own_log_sum_exp: float32 [16, 4096, 32], P('resp', 'ctx'), may hold values from 2 to 9
- prompt_keys: bfloat16 [512, 512], P('ctx'), may hold values from -6 to 6
- prompt_value_rows: bfloat16 [512, 512], P('ctx'), may hold values from -6 to 6
- advantages: float32 [16], P('resp'), may hold values from -3 to 3
- lengths: int32 [16], P('resp'), may hold values from 1024 to 4096, as said below
- mamba_in: bfloat16 [512, 8192], P('ctx', 'resp'), may hold values from -6 to 6
- step_size: float32 [512, 8192], P('ctx', 'resp'), may hold values from 0 to 0.2
- decay_rate: float32 [16, 8192], P(None, 'resp'), may hold values from 0.25 to 4
- input_map: float32 [512, 16], P('ctx'), may hold values from -6 to 6
- output_map: float32 [512, 16], P('ctx'), may hold values from -6 to 6
- mamba_grad: bfloat16 [512, 8192], P('ctx', 'resp'), may hold values from -6 to 6
- state_grad: bfloat16 [16, 16, 8192], P('resp'), may hold values from -24 to 24
Outputs:
- query_grad: bfloat16 [16, 4096, 4096], P('resp', 'ctx')
- key_grad: float32 [512, 512], P('ctx')
- value_grad: float32 [512, 512], P('ctx')
- mamba_input_grad: float32 [512, 8192], P('ctx', 'resp')
- input_map_grad: float32 [512, 16], P('ctx')
The draws below stay inside these ranges and needn't reach their ends.
Inputs may be any that keep to these rules, and one draw needn't show every extreme that they name: `lengths`: some response fills all 4096 positions and some other response has 1024 tokens.
All inputs are finite; a program needn't handle non-finite values.
Results may differ from the reference program's by a relative error of at most 0.02.
Values may be sent and summed in bfloat16 or wider, within the bound.
A program may use at most 64 MiB of HBM per device.

```python
import math
import jax
import jax.numpy as jnp
from jax import lax

QUERY_HEADS = 32
KEY_VALUE_HEADS = 4
HEAD_SIZE = 128
NS = 16
NR = 16
RESPONSE_TOKENS = 4096
PROMPT_TOKENS = 512
CH = 8192


def key_base(key):
    return jnp.clip(jax.random.normal(key, (PROMPT_TOKENS, KEY_VALUE_HEADS * HEAD_SIZE), jnp.float32), -6.0, 6.0)


def draw_prompt_keys(key, part):
    base_offset = key_base(key)
    return base_offset.astype(jnp.bfloat16)


def draw_queries(key, part):
    key = jax.random.fold_in(key, 5)
    raw = jnp.clip(jax.random.normal(key, (NR, RESPONSE_TOKENS, QUERY_HEADS * HEAD_SIZE), jnp.float32), -6.0, 6.0)
    return raw.astype(jnp.bfloat16)


def draw_lengths(key, part):
    key = jax.random.fold_in(key, 9)
    first_key, selection_random_key, other_key = jax.random.split(key, 3)
    counts = jax.random.randint(first_key, (NR,), RESPONSE_TOKENS // 4, RESPONSE_TOKENS + 1)
    longest = jax.random.randint(selection_random_key, (), 0, NR)
    shortest = (longest + 1 + jax.random.randint(other_key, (), 0, NR - 1)) % NR
    counts = counts.at[longest].set(RESPONSE_TOKENS)
    return counts.at[shortest].set(RESPONSE_TOKENS // 4).astype(jnp.int32)


def draw_step_size(key, part):
    key = jax.random.fold_in(key, 7)
    selection_random_key, level_random_key, coarse_random_key, batch_random_key = jax.random.split(key, 4)
    quick = jax.random.randint(selection_random_key, (CH,), 0, 2) == 1
    level = jax.random.uniform(level_random_key, (CH,), jnp.float32)
    slow_step = (0.1 + 0.1 * level) / PROMPT_TOKENS
    quick_step = 0.01 * jnp.exp(jnp.log(3.0) * level)
    channel_stride = jnp.where(quick, quick_step, slow_step)
    coarse_estimate = jax.random.uniform(coarse_random_key, (PROMPT_TOKENS, CH), jnp.float32, 0.5, 1.5)
    sample_positions = jax.random.randint(batch_random_key, (3,), 0, PROMPT_TOKENS)
    draw_batch = jnp.any(jnp.arange(PROMPT_TOKENS, dtype=jnp.int32)[:, None] == sample_positions[None, :], axis=1)
    return channel_stride[None, :] * coarse_estimate + jnp.where(draw_batch, 0.12, 0.0)[:, None]


def with_spikes(array, key, source, target, blocks, factor):
    def block_of(axis_at):
        return (jnp.arange(array.shape[axis_at]) // (array.shape[axis_at] // blocks)).reshape((-1,) + (1,) * (array.ndim - 1 - axis_at))

    first = jax.random.permutation(key, blocks)[block_of(target)]
    other_side = (block_of(target) + blocks // 2) % blocks
    return jnp.where((block_of(source) == first) | (block_of(source) == other_side), factor * array, array)


def levels(rng, dims, cuts, least, largest):
    level = 1.0
    for dim, blocks in cuts:
        heights = jax.random.uniform(jax.random.fold_in(jax.random.fold_in(rng, 6), dim), (blocks,), jnp.float32, least / len(cuts), largest / len(cuts))
        level = level * jnp.repeat(jnp.exp(heights), dims[dim] // blocks).reshape((-1,) + (1,) * (len(dims) - 1 - dim))
    return level


def bell_draw(own_key, extent, scale, limit, shards=(), held_as=jnp.bfloat16):
    factor_of = levels(own_key, extent, shards, -0.22, 0.18) if shards else 1.0
    drawn = jax.random.normal(own_key, extent, jnp.float32) * scale * factor_of
    return jnp.minimum(jnp.maximum(drawn, -limit), limit).astype(held_as)


def heavy_noise(rng, extent, spread, bound, pieces, heavy, kind=jnp.bfloat16):
    result = spread * jax.random.normal(rng, extent, jnp.float32)
    if pieces:
        result = result * levels(rng, extent, pieces, -0.22, 0.18)
    return jnp.clip(with_spikes(result, jax.random.fold_in(rng, 3), *heavy), -bound, bound).astype(kind)


def setup_inputs(seed: int = 0) -> dict:
    streams_of = jax.random.split(jax.random.key(seed), 16)
    return {
        "queries": draw_queries(jax.random.fold_in(streams_of[15], 71), 0),
        "attention_output": bell_draw(streams_of[1], (NR, RESPONSE_TOKENS, QUERY_HEADS * HEAD_SIZE), 1.0, 6.0, ((0, 16), (1, 32))),
        "grad_out": bell_draw(streams_of[2], (NR, RESPONSE_TOKENS, QUERY_HEADS * HEAD_SIZE), 1.0, 6.0, ((0, 16), (1, 32))),
        "own_log_sum_exp": jnp.clip(2.0 + 7.0 * jax.random.uniform(streams_of[3], (NR, RESPONSE_TOKENS, QUERY_HEADS), jnp.float32) ** levels(streams_of[3], (NR, RESPONSE_TOKENS, QUERY_HEADS), ((0, 16), (1, 32)), -0.2, 0.2), 2.0, 9.0),
        "prompt_keys": draw_prompt_keys(jax.random.fold_in(streams_of[15], 71), 0),
        "prompt_value_rows": bell_draw(streams_of[5], (PROMPT_TOKENS, KEY_VALUE_HEADS * HEAD_SIZE), 1.0, 6.0, ((0, 32),)),
        "advantages": bell_draw(streams_of[6], (NR,), 1.0, 3.0, ((0, 16),), jnp.float32),
        "lengths": draw_lengths(jax.random.fold_in(streams_of[15], 71), 0),
        "mamba_in": bell_draw(streams_of[8], (PROMPT_TOKENS, CH), 1.0, 6.0, ((0, 32), (1, 16))),
        "step_size": draw_step_size(jax.random.fold_in(streams_of[15], 71), 0),
        "decay_rate": jnp.clip(jnp.exp(math.log(4.0) - 2.7725887 * jax.random.uniform(streams_of[10], (NS, CH), jnp.float32) ** levels(streams_of[10], (NS, CH), ((1, 16),), -0.2, 0.2)), 0.25, 4.0),
        "input_map": bell_draw(streams_of[11], (PROMPT_TOKENS, NS), 1.0, 6.0, ((0, 32),), jnp.float32),
        "output_map": bell_draw(streams_of[12], (PROMPT_TOKENS, NS), 1.0, 6.0, ((0, 32),), jnp.float32),
        "mamba_grad": bell_draw(streams_of[13], (PROMPT_TOKENS, CH), 1.0, 6.0, ((0, 32), (1, 16))),
        "state_grad": heavy_noise(streams_of[14], (NR, NS, CH), 4.0, 24.0, ((0, 16),), (0, 2, 16, 2.0)),
    }


def contract_last(left, right):
    return lax.dot_general(left, right, (((1,), (1,)), ((), ())), preferred_element_type=jnp.float32)

def contract_first(left, right):
    return lax.dot_general(left, right, (((0,), (0,)), ((), ())), preferred_element_type=jnp.float32)

def prefix_terms(query_rows, grad_rows, output_rows, own_rows, keys_head, values_head, score_scale):
    scores = contract_last(query_rows, keys_head) * score_scale
    row_max = lax.optimization_barrier(jnp.max(scores, axis=1))
    prefix_lse = row_max + jnp.log(lax.optimization_barrier(jnp.sum(jnp.exp(scores - row_max[:, None]), axis=1)))
    larger = jnp.maximum(prefix_lse, own_rows)
    total_lse = larger + jnp.log(jnp.exp(prefix_lse - larger) + jnp.exp(own_rows - larger))
    prob_rows = jnp.exp(scores - total_lse[:, None])
    row_inner = lax.optimization_barrier(jnp.sum(grad_rows.astype(jnp.float32) * output_rows.astype(jnp.float32), axis=1))
    dprob_rows = contract_last(grad_rows, values_head)
    dscores = (prob_rows * (dprob_rows - row_inner[:, None])).astype(jnp.bfloat16)
    return (prob_rows.astype(jnp.bfloat16), dscores)

def reference(queries, attention_output, grad_out, own_log_sum_exp, prompt_keys, prompt_value_rows, advantages, lengths, mamba_in, step_size, decay_rate, input_map, output_map, mamba_grad, state_grad):
    score_scale = 1.0 / math.sqrt(HEAD_SIZE)
    query_group_width = QUERY_HEADS // KEY_VALUE_HEADS
    weight = advantages * jnp.float32(RESPONSE_TOKENS) / lengths.astype(jnp.float32)
    position = jnp.arange(RESPONSE_TOKENS, dtype=jnp.int32)

    def per_response(totals, inputs):
        single_query, single_output, grad_one, single_own_term, weight_one, length_one = inputs
        token_weight = jnp.where(position < length_one, weight_one, jnp.float32(0.0))
        scaled_result = (grad_one.astype(jnp.float32) * token_weight[:, None]).astype(jnp.bfloat16)
        query_pieces = single_query.reshape(RESPONSE_TOKENS, KEY_VALUE_HEADS, query_group_width * HEAD_SIZE)
        output_pieces = single_output.reshape(RESPONSE_TOKENS, KEY_VALUE_HEADS, query_group_width * HEAD_SIZE)
        gradient_pieces = scaled_result.reshape(RESPONSE_TOKENS, KEY_VALUE_HEADS, query_group_width * HEAD_SIZE)
        own_term_pieces = single_own_term.reshape(RESPONSE_TOKENS, KEY_VALUE_HEADS, query_group_width)
        key_parts = []
        value_parts = []
        query_parts = []
        for key_value_head in range(KEY_VALUE_HEADS):
            query_rows = query_pieces[:, key_value_head].reshape(RESPONSE_TOKENS * query_group_width, HEAD_SIZE)
            grad_rows = gradient_pieces[:, key_value_head].reshape(RESPONSE_TOKENS * query_group_width, HEAD_SIZE)
            output_rows = output_pieces[:, key_value_head].reshape(RESPONSE_TOKENS * query_group_width, HEAD_SIZE)
            own_rows = own_term_pieces[:, key_value_head].reshape(RESPONSE_TOKENS * query_group_width)
            keys_head = prompt_keys[:, key_value_head * HEAD_SIZE:(key_value_head + 1) * HEAD_SIZE]
            values_head = prompt_value_rows[:, key_value_head * HEAD_SIZE:(key_value_head + 1) * HEAD_SIZE]
            prob_rows, dscores = prefix_terms(query_rows, grad_rows, output_rows, own_rows, keys_head, values_head, score_scale)
            query_term = jnp.dot(dscores, keys_head, preferred_element_type=jnp.float32) * score_scale
            query_parts.append(query_term.reshape(RESPONSE_TOKENS, query_group_width * HEAD_SIZE))
            key_parts.append(contract_first(dscores, query_rows) * score_scale)
            value_parts.append(contract_first(prob_rows, grad_rows))
        key_total = totals[0] + jnp.concatenate(key_parts, axis=1)
        value_total = totals[1] + jnp.concatenate(value_parts, axis=1)
        return ((key_total, value_total), jnp.concatenate(query_parts, axis=1).astype(jnp.bfloat16))
    empty_key_value = jnp.zeros((PROMPT_TOKENS, KEY_VALUE_HEADS * HEAD_SIZE), jnp.float32)
    (key_grad, value_grad), query_grad = lax.scan(per_response, (empty_key_value, empty_key_value), (queries, attention_output, grad_out, own_log_sum_exp, weight, lengths))
    final_grad = lax.optimization_barrier(jnp.sum(state_grad.astype(jnp.float32), axis=0))

    def backward_step(incoming, inputs):
        step_row, input_row, dy_row, in_map_row, out_map_row = inputs
        adjoint = out_map_row[:, None] * dy_row[None, :] + incoming
        dx_row = step_row * lax.optimization_barrier(jnp.sum(in_map_row[:, None] * adjoint, axis=0))
        db_row = lax.optimization_barrier(jnp.sum(adjoint * (step_row * input_row)[None, :], axis=1))
        return (jnp.exp(-step_row[None, :] * decay_rate) * adjoint, (dx_row, db_row))
    leftover, (mamba_input_grad, input_map_grad) = lax.scan(backward_step, final_grad, (step_size, mamba_in.astype(jnp.float32), mamba_grad.astype(jnp.float32), input_map, output_map), reverse=True)
    return (query_grad, key_grad, value_grad, mamba_input_grad, input_map_grad)
```

```python
import functools
import math

import jax
import jax.numpy as jnp
from jax import lax
from jax.experimental import pallas as pl
from jax.experimental.pallas import tpu as pltpu
from jax.sharding import PartitionSpec as P

X, Y, Z, ZH, ZL, CORES, RESP = 4, 4, 16, 4, 4, 2, 16
GROUP = ZH * CORES
HEADS, KV_HEADS, SIZE = 32, 4, 128
PER_KV = HEADS // KV_HEADS
TOKENS = 128
KEYS = 512
BLOCK = 16
STATE = 16
LANES = 128
CHANNELS = 512
SCALE = 1.0 / math.sqrt(SIZE)
LOG2E = math.log2(math.e)
F32 = jnp.float32
BF16 = jnp.bfloat16
MESH = pl.DeviceIdType.MESH
NT = (((1,), (1,)), ((), ()))
VMEM = pl.BlockSpec(memory_space=pltpu.VMEM)


def place():
    ctx = lax.axis_index("ctx")
    resp = lax.axis_index("resp")
    x = lax.div(ctx, GROUP)
    q = lax.rem(ctx, GROUP)
    zh = lax.div(q, CORES)
    c = lax.rem(q, CORES)
    zl = lax.div(resp, Y)
    y = lax.rem(resp, Y)
    return ctx, resp, x, q, zh, c, zl, y


def step(value, offset, count):
    return lax.rem(value + offset + count, count)


LINE, AY, AX, CORE, STATES, TILES, MAPS, BACKS, SUMS = 0, 1, 2, 3, 5, 6, 7, 8, 9
BX, BY, HALVES = 10, 16, 22
FIRST, SECOND, LINES, PIECES = 26, 30, 34, 36
SEMS = 38


def kernel(
    advantages, lengths, queries_h, outputs_h, grads_h, own_h, keys_h, values_h, mamba_in_h, step_h, rate_h,
    input_map_h, output_map_h, mamba_grad_h, state_h,
    query_grad, key_grad, value_grad, mamba_out, map_out,
    queries, outputs, grads, own, keys, values, mamba_in, step_size, decay_rate, input_map, output_map, mamba_grad,
    state_own, blocks, kv, own_t, inners, square, square_in, decays, tiles_out, tiles_in, state_in,
    group_out, group_in, back_out, back_in, db_out, db_in,
    partial, core_in, pairs, first_in, firsts, second_in, lines, line_in, piece, pieces, query_out,
    load_sem, store_sem, send_sem, recv_sem,
):
    ctx, resp, x, q, zh, c, zl, y = place()
    other = 1 - c
    z = zh * ZL + zl

    xs = [(step(x, d, X) * GROUP + q, resp) for d in range(1, X)]
    ys = [(ctx, zl * Y + step(y, d, Y)) for d in range(1, Y)]
    zs = [(x * GROUP + step(zh, d, ZH) * CORES + c, resp) for d in range(1, ZH)]
    partner = (x * GROUP + zh * CORES + other, resp)

    def group(d):
        return (x * GROUP + step(q, d, GROUP), resp)

    def resps(d):
        return (ctx, step(resp, d, RESP))

    def each(count, act):
        def one(d, carry):
            act(d)
            return carry

        lax.fori_loop(1, count, one, 0)

    mine = pl.multiple_of(resp * CHANNELS + zh * LANES, LANES)
    loads = [
        (keys_h, keys), (values_h, values), (step_h, step_size), (rate_h, decay_rate), (output_map_h, output_map),
        (mamba_grad_h, mamba_grad), (grads_h, grads), (outputs_h, outputs), (own_h, own), (queries_h, queries),
        (mamba_in_h, mamba_in), (input_map_h, input_map), (state_h.at[0, :, pl.ds(mine, LANES)], state_own),
    ]
    loads = [pltpu.make_async_copy(src, dst, load_sem.at[i]) for i, (src, dst) in enumerate(loads)]
    for load in loads:
        load.start()
    wide = PER_KV * SIZE

    def store(g):
        cols = pl.ds(pl.multiple_of(g * wide, wide), wide)
        return pltpu.make_async_copy(query_out.at[0, :, cols], query_grad.at[0, :, cols], store_sem.at[g])

    barrier = pltpu.get_barrier_semaphore()

    def greet(target):
        pl.semaphore_signal(barrier, inc=1, device_id=target, device_id_type=MESH)

    for target in xs:
        greet(target)
    each(GROUP, lambda d: greet(group(d)))
    each(RESP, lambda d: greet(resps(d)))
    for j in range(1, ZL):
        each(ZH, lambda d: greet((x * GROUP + step(zh, d, ZH) * CORES + c, step(zl, j, ZL) * Y + y)))
    partners = 3 + 7 + 15 + 9

    def send(src, dst, target, sem, recv=None):
        pltpu.make_async_remote_copy(
            src_ref=src, dst_ref=dst, send_sem=send_sem.at[sem], recv_sem=recv_sem.at[sem if recv is None else recv],
            device_id=target, device_id_type=MESH,
        ).start()

    def arrived(ref, sem):
        pltpu.make_async_remote_copy(
            src_ref=ref, dst_ref=ref, send_sem=send_sem.at[sem], recv_sem=recv_sem.at[sem],
            device_id=partner, device_id_type=MESH,
        ).wait_recv()

    def left(ref, sem):
        pltpu.make_async_remote_copy(
            src_ref=ref, dst_ref=ref, send_sem=send_sem.at[sem], recv_sem=recv_sem.at[sem],
            device_id=partner, device_id_type=MESH,
        ).wait_send()

    loads[0].wait()
    loads[1].wait()
    for ch in range(2):
        for kind in range(2):
            for gl in range(2):
                g = ch * 2 + gl
                blocks[ch, kind * 2 + gl] = (keys, values)[kind][:, g * LANES:(g + 1) * LANES]
    kv[:, y, c, x, zh] = blocks[:, y]
    pl.semaphore_wait(barrier, partners)
    for d in range(1, ZH):
        send(blocks.at[:, y], kv.at[:, y, c, x, zh], zs[d - 1], LINE)

    for i in range(2, 6):
        loads[i].wait()
    square[...] = jnp.zeros_like(square)
    square[0:16, 0:16] = output_map[...]
    out_t = square[...].T
    rate = decay_rate[...]
    steps = step_size[...]
    dy = mamba_grad[...].astype(F32)
    carry = jnp.zeros((STATE, CHANNELS), F32)
    for t in range(BLOCK - 1, -1, -1):
        decay = jnp.exp(-steps[t:t + 1] * rate)
        decays[t] = decay
        carry = decay * (out_t[0:STATE, t:t + 1] * dy[t:t + 1] + carry)
    span = jnp.exp(-jnp.sum(steps, axis=0, keepdims=True) * rate)
    for k in range(GROUP):
        kt, nh = k // 2, k % 2
        tiles_out[k, 0] = carry[nh * 8:nh * 8 + 8, kt * LANES:(kt + 1) * LANES]
        tiles_out[k, 1] = span[nh * 8:nh * 8 + 8, kt * LANES:(kt + 1) * LANES]
    each(GROUP, lambda d: send(tiles_out.at[step(q, d, GROUP)], tiles_in.at[q], group(d), TILES))
    tiles_in[q] = tiles_out[q]

    arrived(kv.at[:, y, c, x, 0:3], LINE)
    for d in range(1, 4):
        here = kv.at[:, y, c, x, 0:2]
        send(here, here, ys[d - 1], AY)
        here = kv.at[:, y, c, x, 2:4]
        send(here, here, xs[d - 1], AX)

    length = lengths[0]
    weight = advantages[0] * F32(TOKENS * lax.axis_size("ctx")) / length.astype(F32)
    position = ctx * TOKENS + lax.broadcasted_iota(jnp.int32, (TOKENS, 1), 0)
    token_weight = jnp.where(position < length, weight, F32(0.0))
    ones = jnp.ones((8, SIZE), BF16)

    def prepare(quad, carry):
        for i in range(4):
            h = quad * 4 + i
            cols = pl.ds(pl.multiple_of(h * SIZE, SIZE), SIZE)
            scaled = (grads[0, :, cols].astype(F32) * token_weight).astype(BF16)
            grads[0, :, cols] = scaled
            product = scaled.astype(F32) * outputs[0, :, cols].astype(F32)
            high = product.astype(BF16)
            low = (product - high.astype(F32)).astype(BF16)
            inners[h] = (
                lax.dot_general(ones, high, NT, preferred_element_type=F32)
                + lax.dot_general(ones, low, NT, preferred_element_type=F32)
            )
        return carry

    for i in range(6, 9):
        loads[i].wait()
    own_t[...] = own[0] * LOG2E
    lax.fori_loop(0, 4, prepare, 0)

    arrived(kv.at[:, 0:3, c, x, 0:2], AY)
    arrived(kv.at[:, y, c, 0:3, 2:4], AX)
    for ch in range(2):
        by_x = kv.at[ch, :, c, x, 0:2]
        by_y = kv.at[ch, y, c, :, 2:4]
        for d in range(1, 4):
            send(by_x, by_x, xs[d - 1], BX + 3 * ch, BX + 3 * ch + d - 1)
            send(by_y, by_y, ys[d - 1], BY + 3 * ch, BY + 3 * ch + d - 1)
        send(by_x, by_x, partner, CORE + ch)
        send(by_y, by_y, partner, CORE + ch)

    def send_state(d):
        start = pl.multiple_of(step(resp, d, RESP) * CHANNELS + zh * LANES, LANES)
        send(state_h.at[0, :, pl.ds(start, LANES)], state_in.at[d - 1], resps(d), STATES)

    each(RESP, send_state)

    arrived(tiles_in.at[0:7], TILES)
    span_all = jnp.ones((8, LANES), F32)
    carry_all = jnp.zeros((8, LANES), F32)
    for k in range(GROUP - 1, -1, -1):
        carry_all = tiles_in[k, 1] * carry_all + tiles_in[k, 0]
        span_all = span_all * tiles_in[k, 1]
    group_out[0] = carry_all
    group_out[1] = span_all
    for d in range(1, X):
        send(group_out, group_in.at[x], xs[d - 1], MAPS)
    group_in[x] = group_out[...]

    def pass_on(ch):
        for d in range(1, 4):
            here = kv.at[ch, :, c, step(x, -d, X), 0:2]
            arrived(here, BX + 3 * ch + d - 1)
            send(here, here, partner, CORE + ch)
            here = kv.at[ch, step(y, -d, Y), c, :, 2:4]
            arrived(here, BY + 3 * ch + d - 1)
            send(here, here, partner, CORE + ch)

    def carry_back():
        for i in range(10, 13):
            loads[i].wait()
        arrived(state_in.at[0:15], STATES)
        arrived(group_in.at[0:3], MAPS)
        final = state_own[...].astype(F32) + jnp.sum(state_in[...].astype(F32), axis=0)
        incoming = jnp.where(c == 0, final[0:8], final[8:16])
        for k in range(X - 1, 0, -1):
            passed = group_in[k, 1] * incoming + group_in[k, 0]
            incoming = jnp.where(x < k, passed, incoming)
        for k in range(GROUP - 1, -1, -1):
            back_out[k] = incoming
            incoming = tiles_in[k, 1] * incoming + tiles_in[k, 0]
        each(GROUP, lambda d: send(back_out.at[step(q, d, GROUP)], back_in.at[q], group(d), BACKS))
        back_in[q] = back_out[q]

    def rows(ref, pair):
        heads = (2 * pair, 2 * pair + 1)
        return jnp.concatenate([ref[0, :, h * SIZE:(h + 1) * SIZE] for h in heads], axis=0)

    def keys_of(g):
        return kv[g // 2, g % 2].reshape(KEYS, SIZE)

    def begin(pair):
        g = pair // 4
        values_g = kv[g // 2, 2 + g % 2].reshape(KEYS, SIZE)
        scores = lax.dot_general(keys_of(g), rows(queries, pair), NT, preferred_element_type=F32) * (SCALE * LOG2E)
        dprobs = lax.dot_general(values_g, rows(grads, pair), NT, preferred_element_type=F32)
        return scores, dprobs

    def end(pair, begun, transposed, sums):
        scores, dprobs = begun
        h = 2 * pair
        inner = jnp.concatenate([inners[h, 0:1], inners[h + 1, 0:1]], axis=1)
        own2 = jnp.concatenate([own_t[h:h + 1], own_t[h + 1:h + 2]], axis=1)
        top = jnp.maximum(jnp.max(scores, axis=0, keepdims=True), own2)
        powers = jnp.exp2(scores - top)
        total = jnp.sum(powers, axis=0, keepdims=True) + jnp.exp2(own2 - top)
        probs = powers * (1.0 / total)
        dscores = (probs * (dprobs - inner)).astype(BF16)
        query_t = jnp.dot(transposed, dscores, preferred_element_type=F32) * SCALE
        for i in range(2):
            part = query_t[:, i * SIZE:(i + 1) * SIZE].T.astype(BF16)
            query_out[0, :, (h + i) * SIZE:(h + i + 1) * SIZE] = part
        return (
            sums[0] + jnp.dot(dscores, rows(queries, pair), preferred_element_type=F32),
            sums[1] + jnp.dot(probs.astype(BF16), rows(grads, pair), preferred_element_type=F32),
        )

    def ship(g, sums):
        ch, gl = g // 2, g % 2
        for kind in range(2):
            partial[ch, kind, gl] = sums[kind].astype(BF16).reshape(partial.shape[3:])
        send(partial.at[ch, :, gl, other], core_in.at[ch, :, gl], partner, HALVES + g)
        store(g).start()

    def join(g):
        ch, gl = g // 2, g % 2
        arrived(core_in.at[ch, :, gl], HALVES + g)
        for kind in range(2):
            pairs[ch, kind * 2 + gl] = (
                partial[ch, kind, gl, c].astype(F32) + core_in[ch, kind, gl].astype(F32)
            ).astype(BF16)

    def first_hop(ch):
        for d in range(1, 4):
            send(pairs.at[ch, :, step(x, d, X), 0:2], first_in.at[ch, 0, d - 1], xs[d - 1], FIRST + 2 * ch)
            send(pairs.at[ch, step(y, d, Y), :, 2:4], first_in.at[ch, 1, d - 1], ys[d - 1], FIRST + 2 * ch + 1)

    def second_hop(ch):
        for axis in range(2):
            arrived(first_in.at[ch, axis], FIRST + 2 * ch + axis)
            held = pairs[ch, :, x, 0:2] if axis == 0 else pairs[ch, y, :, 2:4]
            total = held.astype(F32)
            for d in range(3):
                total = total + first_in[ch, axis, d].astype(F32)
            firsts[ch, axis] = total.astype(BF16)
            for d in range(1, 4):
                to = step(y, d, Y) if axis == 0 else step(x, d, X)
                target = (ys if axis == 0 else xs)[d - 1]
                send(firsts.at[ch, axis, to], second_in.at[ch, axis, d - 1], target, SECOND + 2 * ch + axis)

    def to_lines(ch):
        for axis in range(2):
            arrived(second_in.at[ch, axis], SECOND + 2 * ch + axis)
            total = firsts[ch, axis, y if axis == 0 else x].astype(F32)
            for d in range(3):
                total = total + second_in[ch, axis, d].astype(F32)
            lines[ch, 2 * axis:2 * axis + 2] = total.astype(BF16)
        for i in range(1, ZH):
            to = step(zh, i, ZH)
            send(lines.at[ch, to], line_in.at[z], (x * GROUP + to * CORES + c, (1 + ch) * Y + y), LINES + ch)

        @pl.when(zl != 1 + ch)
        def _():
            send(lines.at[ch, zh], line_in.at[z], (ctx, (1 + ch) * Y + y), LINES + ch)

    def sum_line(ch):
        @pl.when(zl == 1 + ch)
        def _():
            line_in[z] = lines[ch, zh]
            arrived(line_in.at[0:15], LINES + ch)
            summed = jnp.sum(line_in[...].astype(F32), axis=0)
            piece[...] = summed
            each(RESP, lambda d: send(piece, pieces.at[ch * Y + y], resps(d), PIECES + ch))
            pieces[ch * Y + y] = summed

    loads[9].wait()
    pass_on(0)
    lax.fori_loop(4, 8, prepare, 0)
    arrived(kv.at[0, :, other], CORE)
    begun = begin(0)
    for pair in range(HEADS // 2):
        g = pair // 4
        if pair % 4 == 0:
            transposed = keys_of(g).T
            sums = (jnp.zeros((KEYS, SIZE), F32),) * 2
        if pair == 3:
            pass_on(1)
        if pair == 7:
            arrived(kv.at[1, :, other], CORE + 1)
        ahead = begin(pair + 1) if pair + 1 < HEADS // 2 else None
        sums = end(pair, begun, transposed, sums)
        begun = ahead
        if pair % 4 == 3:
            ship(g, sums)
            if g == 1:
                join(0)
                carry_back()
            if g == 2:
                join(1)
                first_hop(0)
    join(2)
    second_hop(0)
    join(3)
    first_hop(1)
    to_lines(0)

    arrived(back_in.at[0:7], BACKS)
    square_in[...] = jnp.zeros_like(square_in)
    square_in[0:16, 0:16] = input_map[...]
    in_t = square_in[...].T
    taken = steps * mamba_in[...].astype(F32)
    carry = jnp.concatenate(
        [jnp.concatenate([back_in[kt * 2 + nh] for kt in range(4)], axis=1) for nh in range(2)], axis=0
    )
    lane = lax.broadcasted_iota(jnp.int32, (STATE, LANES), 1)
    db = jnp.zeros((STATE, LANES), F32)
    for t in range(BLOCK - 1, -1, -1):
        adjoint = out_t[0:STATE, t:t + 1] * dy[t:t + 1] + carry
        total = jnp.sum(in_t[0:STATE, t:t + 1] * adjoint, axis=0, keepdims=True)
        mamba_out[t:t + 1, :] = steps[t:t + 1] * total
        term = adjoint * taken[t:t + 1]
        term = (term[:, 0:128] + term[:, 128:256]) + (term[:, 256:384] + term[:, 384:512])
        db = jnp.where(lane == t, jnp.sum(term, axis=1, keepdims=True), db)
        carry = decays[t] * adjoint
    db_out[...] = db

    second_hop(1)
    each(RESP, lambda d: send(db_out, db_in.at[d - 1], resps(d), SUMS))
    to_lines(1)
    sum_line(0)
    arrived(db_in.at[0:15], SUMS)
    square[0:STATE, :] = db_out[...] + jnp.sum(db_in[...], axis=0)
    map_out[...] = square[...].T[0:16, 0:16]
    sum_line(1)

    left(blocks.at[:, 0:3], LINE)
    left(tiles_out.at[0:7], TILES)
    left(kv.at[:, 0:3, c, x, 0:2], AY)
    left(kv.at[:, y, c, 0:3, 2:4], AX)
    left(state_in.at[0:15], STATES)
    for ch in range(2):
        left(kv.at[ch, :, c, 0:3, 0:2], BX + 3 * ch)
        left(kv.at[ch, 0:3, c, :, 2:4], BY + 3 * ch)
        left(kv.at[ch, :, c], CORE + ch)
    left(group_in.at[0:3], MAPS)
    left(back_out.at[0:7], BACKS)
    for g in range(KV_HEADS):
        left(core_in.at[g // 2, :, g % 2], HALVES + g)
    for ch in range(2):
        for axis in range(2):
            left(first_in.at[ch, axis], FIRST + 2 * ch + axis)
            left(second_in.at[ch, axis], SECOND + 2 * ch + axis)
    left(db_in.at[0:15], SUMS)
    for ch in range(2):

        @pl.when(zl == 1 + ch)
        def _():
            left(line_in.at[0:3], LINES + ch)
            left(db_in.at[0:15], PIECES + ch)

        @pl.when(zl != 1 + ch)
        def _():
            left(line_in.at[0:4], LINES + ch)

    for g in range(KV_HEADS):
        store(g).wait()

    for ch in range(2):

        @pl.when(zl == 1 + ch)
        def _():
            arrived(pieces.at[0:3], PIECES + ch)

        @pl.when(zl != 1 + ch)
        def _():
            arrived(pieces.at[0:4], PIECES + ch)

        for gl in range(2):
            cols = slice((ch * 2 + gl) * LANES, (ch * 2 + gl + 1) * LANES)
            key_grad[:, cols] = pieces[ch * Y + gl] * SCALE
            value_grad[:, cols] = pieces[ch * Y + 2 + gl]


def finish_kernel(*refs):
    given, results, held = refs[0:5], refs[5:10], refs[10:15]
    sem_in, sem_out = refs[15], refs[16]
    part = (given[0].at[0], held[0].at[0], results[0].at[0])
    moves = [(given[i], held[i], results[i]) for i in range(1, 5)]
    for i in range(8):
        rows = slice(i * BLOCK, (i + 1) * BLOCK)
        moves.append(tuple(ref.at[rows] for ref in part))
    copies_in = [pltpu.make_async_copy(src, mid, sem_in.at[i]) for i, (src, mid, _) in enumerate(moves)]
    copies_out = [pltpu.make_async_copy(mid, dst, sem_out.at[i]) for i, (_, mid, dst) in enumerate(moves)]
    for copy in copies_in:
        copy.start()
    for first, then in zip(copies_in, copies_out):
        first.wait()
        then.start()
    for copy in copies_out:
        copy.wait()


def on_device(
    queries, attention_output, grad_out, own_log_sum_exp, prompt_keys, prompt_value_rows, advantages, lengths,
    mamba_in, step_size, decay_rate, input_map, output_map, mamba_grad, state_grad,
):
    smem = pl.BlockSpec(memory_space=pltpu.SMEM)
    anywhere = pl.BlockSpec(memory_space=pl.ANY)
    tile = (ZH, BLOCK, LANES)
    half = (2, BLOCK, LANES)
    wide = (1, TOKENS, HEADS * SIZE)
    block_grad = jax.ShapeDtypeStruct((BLOCK, KV_HEADS * SIZE), F32)
    results = (
        jax.ShapeDtypeStruct(wide, BF16),
        block_grad,
        block_grad,
        jax.ShapeDtypeStruct((BLOCK, CHANNELS), F32),
        jax.ShapeDtypeStruct((BLOCK, STATE), F32),
    )
    computed = pl.pallas_call(
        kernel,
        out_shape=results,
        in_specs=[smem] * 2 + [anywhere] * 13,
        out_specs=(anywhere,) + (VMEM,) * 4,
        scratch_shapes=[
            pltpu.VMEM(wide, BF16),
            pltpu.VMEM(wide, BF16),
            pltpu.VMEM(wide, BF16),
            pltpu.VMEM((1, HEADS, TOKENS), F32),
            pltpu.VMEM((BLOCK, KV_HEADS * SIZE), BF16),
            pltpu.VMEM((BLOCK, KV_HEADS * SIZE), BF16),
            pltpu.VMEM((BLOCK, CHANNELS), BF16),
            pltpu.VMEM((BLOCK, CHANNELS), F32),
            pltpu.VMEM((STATE, CHANNELS), F32),
            pltpu.VMEM((BLOCK, STATE), F32),
            pltpu.VMEM((BLOCK, STATE), F32),
            pltpu.VMEM((BLOCK, CHANNELS), BF16),
            pltpu.VMEM((STATE, LANES), BF16),
            pltpu.VMEM((2, 4, BLOCK, LANES), BF16),
            pltpu.VMEM((2, 4, CORES, X) + tile, BF16),
            pltpu.VMEM((HEADS, TOKENS), F32),
            pltpu.VMEM((HEADS, 8, TOKENS), F32),
            pltpu.VMEM((LANES, LANES), F32),
            pltpu.VMEM((LANES, LANES), F32),
            pltpu.VMEM((BLOCK, STATE, CHANNELS), F32),
            pltpu.VMEM((GROUP, 2, 8, LANES), F32),
            pltpu.VMEM((GROUP, 2, 8, LANES), F32),
            pltpu.VMEM((RESP - 1, STATE, LANES), BF16),
            pltpu.VMEM((2, 8, LANES), F32),
            pltpu.VMEM((X, 2, 8, LANES), F32),
            pltpu.VMEM((GROUP, 8, LANES), F32),
            pltpu.VMEM((GROUP, 8, LANES), F32),
            pltpu.VMEM((STATE, LANES), F32),
            pltpu.VMEM((RESP - 1, STATE, LANES), F32),
            pltpu.VMEM((2, 2, 2, CORES, X) + tile, BF16),
            pltpu.VMEM((2, 2, 2, X) + tile, BF16),
            pltpu.VMEM((2, 4, X) + tile, BF16),
            pltpu.VMEM((2, 2, 3, 4) + half, BF16),
            pltpu.VMEM((2, 2, 4) + half, BF16),
            pltpu.VMEM((2, 2, 3) + half, BF16),
            pltpu.VMEM((2,) + tile, BF16),
            pltpu.VMEM((Z, BLOCK, LANES), BF16),
            pltpu.VMEM((BLOCK, LANES), F32),
            pltpu.VMEM((2 * Y, BLOCK, LANES), F32),
            pltpu.VMEM(wide, BF16),
            pltpu.SemaphoreType.DMA((13,)),
            pltpu.SemaphoreType.DMA((KV_HEADS,)),
            pltpu.SemaphoreType.DMA((SEMS,)),
            pltpu.SemaphoreType.DMA((SEMS,)),
        ],
        compiler_params=pltpu.CompilerParams(
            collective_id=0, has_side_effects=True, vmem_limit_bytes=56 * 2**20
        ),
        name="whole",
    )(
        advantages, lengths, queries, attention_output, grad_out, jnp.swapaxes(own_log_sum_exp, 1, 2), prompt_keys,
        prompt_value_rows, mamba_in, step_size, decay_rate, input_map, output_map, mamba_grad, state_grad,
    )
    return pl.pallas_call(
        finish_kernel,
        out_shape=results,
        in_specs=[anywhere] * 5,
        out_specs=(anywhere,) * 5,
        scratch_shapes=[pltpu.VMEM(r.shape, r.dtype) for r in results]
        + [pltpu.SemaphoreType.DMA((12,)), pltpu.SemaphoreType.DMA((12,))],
        compiler_params=pltpu.CompilerParams(vmem_limit_bytes=60 * 2**20),
        name="finish",
    )(*computed)


def solution(mesh):
    placed = (
        P("resp", "ctx", None),
        P("resp", "ctx", None),
        P("resp", "ctx", None),
        P("resp", "ctx", None),
        P("ctx", None),
        P("ctx", None),
        P("resp"),
        P("resp"),
        P("ctx", "resp"),
        P("ctx", "resp"),
        P(None, "resp"),
        P("ctx", None),
        P("ctx", None),
        P("ctx", "resp"),
        P("resp", None, None),
    )
    return jax.shard_map(
        on_device,
        mesh=mesh,
        in_specs=placed,
        out_specs=(
            P("resp", "ctx", None),
            P("ctx", None),
            P("ctx", None),
            P("ctx", "resp"),
            P("ctx", None),
        ),
        check_vma=False,
    )
```

```python
import functools
import math

import jax
import jax.numpy as jnp
from jax import lax
from jax.experimental import pallas as pl
from jax.experimental.pallas import tpu as pltpu
from jax.sharding import PartitionSpec as P

X, Y, Z, ZH, ZL, CORES, RESP = 4, 4, 16, 4, 4, 2, 16
GROUP = ZH * CORES
HEADS, KV_HEADS, SIZE = 32, 4, 128
PER_KV = HEADS // KV_HEADS
TOKENS = 128
KEYS = 512
BLOCK = 16
STATE = 16
LANES = 128
CHANNELS = 512
SCALE = 1.0 / math.sqrt(SIZE)
LOG2E = math.log2(math.e)
F32 = jnp.float32
BF16 = jnp.bfloat16
MESH = pl.DeviceIdType.MESH
NT = (((1,), (1,)), ((), ()))
VMEM = pl.BlockSpec(memory_space=pltpu.VMEM)


def place():
    ctx = lax.axis_index("ctx")
    resp = lax.axis_index("resp")
    x = lax.div(ctx, GROUP)
    q = lax.rem(ctx, GROUP)
    zh = lax.div(q, CORES)
    c = lax.rem(q, CORES)
    zl = lax.div(resp, Y)
    y = lax.rem(resp, Y)
    return ctx, resp, x, q, zh, c, zl, y


def step(value, offset, count):
    return lax.rem(value + offset + count, count)


LINE, AY, AX, CORE, STATES, TILES, MAPS, BACKS, SUMS = 0, 3, 4, 5, 8, 9, 10, 11, 12
BX, BY, HALVES = 13, 22, 25
FIRST, SECOND, LINES, PIECES = 29, 33, 37, 39
SEMS = 41


def kernel(
    advantages, lengths, queries_h, outputs_h, grads_h, own_h, keys_h, values_h, mamba_in_h, step_h, rate_h,
    input_map_h, output_map_h, mamba_grad_h, state_h,
    query_grad, key_grad, value_grad, mamba_out, map_out,
    queries, outputs, grads, own, keys, values, mamba_in, step_size, decay_rate, input_map, output_map, mamba_grad,
    state_own, blocks, kv, own_t, inners, square, square_in, decays, tiles_out, tiles_in, state_in,
    group_out, group_in, back_out, back_in, db_out, db_in,
    partial, core_in, pairs, first_in, firsts, second_in, lines, line_in, piece, pieces, query_out,
    load_sem, store_sem, send_sem, recv_sem,
):
    ctx, resp, x, q, zh, c, zl, y = place()
    other = 1 - c
    yk, yg = lax.div(y, 2), lax.rem(y, 2)
    z = zh * ZL + zl

    xs = [(step(x, d, X) * GROUP + q, resp) for d in range(1, X)]
    ys = [(ctx, zl * Y + step(y, d, Y)) for d in range(1, Y)]
    zs = [(x * GROUP + step(zh, d, ZH) * CORES + c, resp) for d in range(1, ZH)]
    partner = (x * GROUP + zh * CORES + other, resp)

    def group(d):
        return (x * GROUP + step(q, d, GROUP), resp)

    def resps(d):
        return (ctx, step(resp, d, RESP))

    def each(count, act):
        def one(d, carry):
            act(d)
            return carry

        lax.fori_loop(1, count, one, 0)

    mine = pl.multiple_of(resp * CHANNELS + zh * LANES, LANES)
    loads = [
        (keys_h, keys), (values_h, values), (step_h, step_size), (rate_h, decay_rate), (output_map_h, output_map),
        (mamba_grad_h, mamba_grad), (grads_h, grads), (outputs_h, outputs), (own_h, own), (queries_h, queries),
        (mamba_in_h, mamba_in), (input_map_h, input_map), (state_h.at[0, :, pl.ds(mine, LANES)], state_own),
    ]
    loads = [pltpu.make_async_copy(src, dst, load_sem.at[i]) for i, (src, dst) in enumerate(loads)]
    for load in loads:
        load.start()
    wide = PER_KV * SIZE

    def store(g):
        cols = pl.ds(pl.multiple_of(g * wide, wide), wide)
        return pltpu.make_async_copy(query_out.at[0, :, cols], query_grad.at[0, :, cols], store_sem.at[g])

    barrier = pltpu.get_barrier_semaphore()

    def greet(target):
        pl.semaphore_signal(barrier, inc=1, device_id=target, device_id_type=MESH)

    for target in xs:
        greet(target)
    each(GROUP, lambda d: greet(group(d)))
    each(RESP, lambda d: greet(resps(d)))
    for j in range(1, ZL):
        each(ZH, lambda d: greet((x * GROUP + step(zh, d, ZH) * CORES + c, step(zl, j, ZL) * Y + y)))
    partners = 3 + 7 + 15 + 9

    def send(src, dst, target, sem, recv=None):
        pltpu.make_async_remote_copy(
            src_ref=src, dst_ref=dst, send_sem=send_sem.at[sem], recv_sem=recv_sem.at[sem if recv is None else recv],
            device_id=target, device_id_type=MESH,
        ).start()

    def arrived(ref, sem):
        pltpu.make_async_remote_copy(
            src_ref=ref, dst_ref=ref, send_sem=send_sem.at[sem], recv_sem=recv_sem.at[sem],
            device_id=partner, device_id_type=MESH,
        ).wait_recv()

    def left(ref, sem):
        pltpu.make_async_remote_copy(
            src_ref=ref, dst_ref=ref, send_sem=send_sem.at[sem], recv_sem=recv_sem.at[sem],
            device_id=partner, device_id_type=MESH,
        ).wait_send()

    loads[0].wait()
    loads[1].wait()
    for ch in range(2):
        for kind in range(2):
            for gl in range(2):
                g = ch * 2 + gl
                blocks[ch, kind, gl] = (keys, values)[kind][:, g * LANES:(g + 1) * LANES]
    kv[0, :, :, c, x, zh] = blocks[0]
    kv[1, yk, yg, c, x, zh] = blocks[1, yk, yg]
    pl.semaphore_wait(barrier, partners)
    for gl in range(2):
        for d in range(1, ZH):
            send(blocks.at[0, :, gl], kv.at[0, :, gl, c, x, zh], zs[d - 1], LINE + gl)
    for d in range(1, ZH):
        send(blocks.at[1, yk, yg], kv.at[1, yk, yg, c, x, zh], zs[d - 1], LINE + 2)

    for i in range(2, 6):
        loads[i].wait()
    square[...] = jnp.zeros_like(square)
    square[0:16, 0:16] = output_map[...]
    out_t = square[...].T
    rate = decay_rate[...]
    steps = step_size[...]
    dy = mamba_grad[...].astype(F32)
    carry = jnp.zeros((STATE, CHANNELS), F32)
    for t in range(BLOCK - 1, -1, -1):
        decay = jnp.exp(-steps[t:t + 1] * rate)
        decays[t] = decay
        carry = decay * (out_t[0:STATE, t:t + 1] * dy[t:t + 1] + carry)
    span = jnp.exp(-jnp.sum(steps, axis=0, keepdims=True) * rate)
    for k in range(GROUP):
        kt, nh = k // 2, k % 2
        tiles_out[k, 0] = carry[nh * 8:nh * 8 + 8, kt * LANES:(kt + 1) * LANES]
        tiles_out[k, 1] = span[nh * 8:nh * 8 + 8, kt * LANES:(kt + 1) * LANES]
    each(GROUP, lambda d: send(tiles_out.at[step(q, d, GROUP)], tiles_in.at[q], group(d), TILES))
    tiles_in[q] = tiles_out[q]

    for gl in range(2):
        arrived(kv.at[0, :, gl, c, x, 0:3], LINE + gl)
        here = kv.at[0, :, gl, c, x]
        for d in range(1, 4):
            send(here, here, xs[d - 1], BX + 3 * gl, BX + 3 * gl + d - 1)
        send(here, here, partner, CORE + gl)
    arrived(kv.at[1, yk, yg, c, x, 0:3], LINE + 2)
    for d in range(1, 4):
        here = kv.at[1, yk, yg, c, x, 0:2]
        send(here, here, ys[d - 1], AY)
        here = kv.at[1, yk, yg, c, x, 2:4]
        send(here, here, xs[d - 1], AX)

    def send_state(d):
        start = pl.multiple_of(step(resp, d, RESP) * CHANNELS + zh * LANES, LANES)
        send(state_h.at[0, :, pl.ds(start, LANES)], state_in.at[d - 1], resps(d), STATES)

    each(RESP, send_state)

    length = lengths[0]
    weight = advantages[0] * F32(TOKENS * lax.axis_size("ctx")) / length.astype(F32)
    position = ctx * TOKENS + lax.broadcasted_iota(jnp.int32, (TOKENS, 1), 0)
    token_weight = jnp.where(position < length, weight, F32(0.0))
    ones = jnp.ones((8, SIZE), BF16)

    def prepare(quad, carry):
        for i in range(4):
            h = quad * 4 + i
            cols = pl.ds(pl.multiple_of(h * SIZE, SIZE), SIZE)
            scaled = (grads[0, :, cols].astype(F32) * token_weight).astype(BF16)
            grads[0, :, cols] = scaled
            product = scaled.astype(F32) * outputs[0, :, cols].astype(F32)
            high = product.astype(BF16)
            low = (product - high.astype(F32)).astype(BF16)
            inners[h] = (
                lax.dot_general(ones, high, NT, preferred_element_type=F32)
                + lax.dot_general(ones, low, NT, preferred_element_type=F32)
            )
        return carry

    for i in range(6, 9):
        loads[i].wait()
    own_t[...] = own[0] * LOG2E
    lax.fori_loop(0, 4, prepare, 0)

    arrived(tiles_in.at[0:7], TILES)
    span_all = jnp.ones((8, LANES), F32)
    carry_all = jnp.zeros((8, LANES), F32)
    for k in range(GROUP - 1, -1, -1):
        carry_all = tiles_in[k, 1] * carry_all + tiles_in[k, 0]
        span_all = span_all * tiles_in[k, 1]
    group_out[0] = carry_all
    group_out[1] = span_all
    for d in range(1, X):
        send(group_out, group_in.at[x], xs[d - 1], MAPS)
    group_in[x] = group_out[...]

    def second_gather():
        by_x = kv.at[1, :, :, c, x, 0:2]
        by_y = kv.at[1, yk, yg, c, :, 2:4]
        arrived(kv.at[1, 0, 0, c, 0:3, 0:2], AY)
        arrived(kv.at[1, 0, 0, c, 0:3, 2:4], AX)
        for d in range(1, 4):
            send(by_x, by_x, xs[d - 1], BX + 6, BX + 6 + d - 1)
            send(by_y, by_y, ys[d - 1], BY, BY + d - 1)
        send(by_x, by_x, partner, CORE + 2)
        send(by_y, by_y, partner, CORE + 2)

    def pass_head(gl):
        for d in range(1, 4):
            here = kv.at[0, :, gl, c, step(x, -d, X)]
            arrived(here, BX + 3 * gl + d - 1)
            send(here, here, partner, CORE + gl)

    def pass_chunk():
        for d in range(1, 4):
            here = kv.at[1, :, :, c, step(x, -d, X), 0:2]
            arrived(here, BX + 6 + d - 1)
            send(here, here, partner, CORE + 2)
            from_y = step(y, -d, Y)
            here = kv.at[1, lax.div(from_y, 2), lax.rem(from_y, 2), c, :, 2:4]
            arrived(here, BY + d - 1)
            send(here, here, partner, CORE + 2)

    def carry_back():
        for i in range(10, 13):
            loads[i].wait()
        arrived(state_in.at[0:15], STATES)
        arrived(group_in.at[0:3], MAPS)
        final = state_own[...].astype(F32) + jnp.sum(state_in[...].astype(F32), axis=0)
        incoming = jnp.where(c == 0, final[0:8], final[8:16])
        for k in range(X - 1, 0, -1):
            passed = group_in[k, 1] * incoming + group_in[k, 0]
            incoming = jnp.where(x < k, passed, incoming)
        for k in range(GROUP - 1, -1, -1):
            back_out[k] = incoming
            incoming = tiles_in[k, 1] * incoming + tiles_in[k, 0]
        each(GROUP, lambda d: send(back_out.at[step(q, d, GROUP)], back_in.at[q], group(d), BACKS))
        back_in[q] = back_out[q]

    def rows(ref, pair):
        heads = (2 * pair, 2 * pair + 1)
        return jnp.concatenate([ref[0, :, h * SIZE:(h + 1) * SIZE] for h in heads], axis=0)

    def keys_of(g):
        return kv[g // 2, 0, g % 2].reshape(KEYS, SIZE)

    def begin(pair):
        g = pair // 4
        values_g = kv[g // 2, 1, g % 2].reshape(KEYS, SIZE)
        scores = lax.dot_general(keys_of(g), rows(queries, pair), NT, preferred_element_type=F32) * (SCALE * LOG2E)
        dprobs = lax.dot_general(values_g, rows(grads, pair), NT, preferred_element_type=F32)
        return scores, dprobs

    def end(pair, begun, transposed, sums):
        scores, dprobs = begun
        h = 2 * pair
        inner = jnp.concatenate([inners[h, 0:1], inners[h + 1, 0:1]], axis=1)
        own2 = jnp.concatenate([own_t[h:h + 1], own_t[h + 1:h + 2]], axis=1)
        top = jnp.maximum(jnp.max(scores, axis=0, keepdims=True), own2)
        powers = jnp.exp2(scores - top)
        total = jnp.sum(powers, axis=0, keepdims=True) + jnp.exp2(own2 - top)
        probs = powers * (1.0 / total)
        dscores = (probs * (dprobs - inner)).astype(BF16)
        query_t = jnp.dot(transposed, dscores, preferred_element_type=F32) * SCALE
        for i in range(2):
            part = query_t[:, i * SIZE:(i + 1) * SIZE].T.astype(BF16)
            query_out[0, :, (h + i) * SIZE:(h + i + 1) * SIZE] = part
        return (
            sums[0] + jnp.dot(dscores, rows(queries, pair), preferred_element_type=F32),
            sums[1] + jnp.dot(probs.astype(BF16), rows(grads, pair), preferred_element_type=F32),
        )

    def ship(g, sums):
        ch, gl = g // 2, g % 2
        for kind in range(2):
            partial[ch, kind, gl] = sums[kind].astype(BF16).reshape(partial.shape[3:])
        send(partial.at[ch, :, gl, other], core_in.at[ch, :, gl], partner, HALVES + g)
        store(g).start()

    def join(g):
        ch, gl = g // 2, g % 2
        arrived(core_in.at[ch, :, gl], HALVES + g)
        for kind in range(2):
            pairs[ch, kind * 2 + gl] = (
                partial[ch, kind, gl, c].astype(F32) + core_in[ch, kind, gl].astype(F32)
            ).astype(BF16)

    def first_hop(ch):
        for d in range(1, 4):
            send(pairs.at[ch, :, step(x, d, X), 0:2], first_in.at[ch, 0, d - 1], xs[d - 1], FIRST + 2 * ch)
            send(pairs.at[ch, step(y, d, Y), :, 2:4], first_in.at[ch, 1, d - 1], ys[d - 1], FIRST + 2 * ch + 1)

    def second_hop(ch):
        for axis in range(2):
            arrived(first_in.at[ch, axis], FIRST + 2 * ch + axis)
            held = pairs[ch, :, x, 0:2] if axis == 0 else pairs[ch, y, :, 2:4]
            total = held.astype(F32)
            for d in range(3):
                total = total + first_in[ch, axis, d].astype(F32)
            firsts[ch, axis] = total.astype(BF16)
            for d in range(1, 4):
                to = step(y, d, Y) if axis == 0 else step(x, d, X)
                target = (ys if axis == 0 else xs)[d - 1]
                send(firsts.at[ch, axis, to], second_in.at[ch, axis, d - 1], target, SECOND + 2 * ch + axis)

    def to_lines(ch):
        for axis in range(2):
            arrived(second_in.at[ch, axis], SECOND + 2 * ch + axis)
            total = firsts[ch, axis, y if axis == 0 else x].astype(F32)
            for d in range(3):
                total = total + second_in[ch, axis, d].astype(F32)
            lines[ch, 2 * axis:2 * axis + 2] = total.astype(BF16)
        for i in range(1, ZH):
            to = step(zh, i, ZH)
            send(lines.at[ch, to], line_in.at[z], (x * GROUP + to * CORES + c, (1 + ch) * Y + y), LINES + ch)

        @pl.when(zl != 1 + ch)
        def _():
            send(lines.at[ch, zh], line_in.at[z], (ctx, (1 + ch) * Y + y), LINES + ch)

    def sum_line(ch):
        @pl.when(zl == 1 + ch)
        def _():
            line_in[z] = lines[ch, zh]
            arrived(line_in.at[0:15], LINES + ch)
            summed = jnp.sum(line_in[...].astype(F32), axis=0)
            piece[...] = summed
            each(RESP, lambda d: send(piece, pieces.at[ch * Y + y], resps(d), PIECES + ch))
            pieces[ch * Y + y] = summed

    loads[9].wait()
    pass_head(0)
    second_gather()
    lax.fori_loop(4, 8, prepare, 0)
    pass_head(1)
    arrived(kv.at[0, :, 0, other], CORE)
    begun = begin(0)
    for pair in range(HEADS // 2):
        g = pair // 4
        if pair % 4 == 0:
            transposed = keys_of(g).T
            sums = (jnp.zeros((KEYS, SIZE), F32),) * 2
        if pair == 3:
            arrived(kv.at[0, :, 1, other], CORE + 1)
        if pair == 4:
            pass_chunk()
        if pair == 7:
            arrived(kv.at[1, :, :, other], CORE + 2)
        ahead = begin(pair + 1) if pair + 1 < HEADS // 2 else None
        sums = end(pair, begun, transposed, sums)
        begun = ahead
        if pair % 4 == 3:
            ship(g, sums)
            if g == 1:
                join(0)
                carry_back()
            if g == 2:
                join(1)
                first_hop(0)
    join(2)
    second_hop(0)
    join(3)
    first_hop(1)
    to_lines(0)

    arrived(back_in.at[0:7], BACKS)
    square_in[...] = jnp.zeros_like(square_in)
    square_in[0:16, 0:16] = input_map[...]
    in_t = square_in[...].T
    taken = steps * mamba_in[...].astype(F32)
    carry = jnp.concatenate(
        [jnp.concatenate([back_in[kt * 2 + nh] for kt in range(4)], axis=1) for nh in range(2)], axis=0
    )
    lane = lax.broadcasted_iota(jnp.int32, (STATE, LANES), 1)
    db = jnp.zeros((STATE, LANES), F32)
    for t in range(BLOCK - 1, -1, -1):
        adjoint = out_t[0:STATE, t:t + 1] * dy[t:t + 1] + carry
        total = jnp.sum(in_t[0:STATE, t:t + 1] * adjoint, axis=0, keepdims=True)
        mamba_out[t:t + 1, :] = steps[t:t + 1] * total
        term = adjoint * taken[t:t + 1]
        term = (term[:, 0:128] + term[:, 128:256]) + (term[:, 256:384] + term[:, 384:512])
        db = jnp.where(lane == t, jnp.sum(term, axis=1, keepdims=True), db)
        carry = decays[t] * adjoint
    db_out[...] = db

    second_hop(1)
    each(RESP, lambda d: send(db_out, db_in.at[d - 1], resps(d), SUMS))
    to_lines(1)
    sum_line(0)
    arrived(db_in.at[0:15], SUMS)
    square[0:STATE, :] = db_out[...] + jnp.sum(db_in[...], axis=0)
    map_out[...] = square[...].T[0:16, 0:16]
    sum_line(1)

    for gl in range(2):
        left(kv.at[0, :, gl, c, x, 0:3], LINE + gl)
        left(kv.at[0, :, gl, c, 0:3], BX + 3 * gl)
        left(kv.at[0, :, gl, c], CORE + gl)
    left(kv.at[1, 0, 0, c, x, 0:3], LINE + 2)
    left(tiles_out.at[0:7], TILES)
    left(kv.at[1, 0, 0, c, 0:3, 0:2], AY)
    left(kv.at[1, 0, 0, c, 0:3, 2:4], AX)
    left(kv.at[1, :, :, c, 0:3, 0:2], BX + 6)
    left(kv.at[0, :, 0, c, 0:3], BY)
    left(kv.at[1, :, :, c], CORE + 2)
    left(state_in.at[0:15], STATES)
    left(group_in.at[0:3], MAPS)
    left(back_out.at[0:7], BACKS)
    for g in range(KV_HEADS):
        left(core_in.at[g // 2, :, g % 2], HALVES + g)
    for ch in range(2):
        for axis in range(2):
            left(first_in.at[ch, axis], FIRST + 2 * ch + axis)
            left(second_in.at[ch, axis], SECOND + 2 * ch + axis)
    left(db_in.at[0:15], SUMS)
    for ch in range(2):

        @pl.when(zl == 1 + ch)
        def _():
            left(line_in.at[0:3], LINES + ch)
            left(db_in.at[0:15], PIECES + ch)

        @pl.when(zl != 1 + ch)
        def _():
            left(line_in.at[0:4], LINES + ch)

    for g in range(KV_HEADS):
        store(g).wait()

    for ch in range(2):

        @pl.when(zl == 1 + ch)
        def _():
            arrived(pieces.at[0:3], PIECES + ch)

        @pl.when(zl != 1 + ch)
        def _():
            arrived(pieces.at[0:4], PIECES + ch)

        for gl in range(2):
            cols = slice((ch * 2 + gl) * LANES, (ch * 2 + gl + 1) * LANES)
            key_grad[:, cols] = pieces[ch * Y + gl] * SCALE
            value_grad[:, cols] = pieces[ch * Y + 2 + gl]


def finish_kernel(*refs):
    given, results, held = refs[0:5], refs[5:10], refs[10:15]
    sem_in, sem_out = refs[15], refs[16]
    part = (given[0].at[0], held[0].at[0], results[0].at[0])
    moves = [(given[i], held[i], results[i]) for i in range(1, 5)]
    for i in range(8):
        rows = slice(i * BLOCK, (i + 1) * BLOCK)
        moves.append(tuple(ref.at[rows] for ref in part))
    copies_in = [pltpu.make_async_copy(src, mid, sem_in.at[i]) for i, (src, mid, _) in enumerate(moves)]
    copies_out = [pltpu.make_async_copy(mid, dst, sem_out.at[i]) for i, (_, mid, dst) in enumerate(moves)]
    for copy in copies_in:
        copy.start()
    for first, then in zip(copies_in, copies_out):
        first.wait()
        then.start()
    for copy in copies_out:
        copy.wait()


def on_device(
    queries, attention_output, grad_out, own_log_sum_exp, prompt_keys, prompt_value_rows, advantages, lengths,
    mamba_in, step_size, decay_rate, input_map, output_map, mamba_grad, state_grad,
):
    smem = pl.BlockSpec(memory_space=pltpu.SMEM)
    anywhere = pl.BlockSpec(memory_space=pl.ANY)
    tile = (ZH, BLOCK, LANES)
    half = (2, BLOCK, LANES)
    wide = (1, TOKENS, HEADS * SIZE)
    block_grad = jax.ShapeDtypeStruct((BLOCK, KV_HEADS * SIZE), F32)
    results = (
        jax.ShapeDtypeStruct(wide, BF16),
        block_grad,
        block_grad,
        jax.ShapeDtypeStruct((BLOCK, CHANNELS), F32),
        jax.ShapeDtypeStruct((BLOCK, STATE), F32),
    )
    computed = pl.pallas_call(
        kernel,
        out_shape=results,
        in_specs=[smem] * 2 + [anywhere] * 13,
        out_specs=(anywhere,) + (VMEM,) * 4,
        scratch_shapes=[
            pltpu.VMEM(wide, BF16),
            pltpu.VMEM(wide, BF16),
            pltpu.VMEM(wide, BF16),
            pltpu.VMEM((1, HEADS, TOKENS), F32),
            pltpu.VMEM((BLOCK, KV_HEADS * SIZE), BF16),
            pltpu.VMEM((BLOCK, KV_HEADS * SIZE), BF16),
            pltpu.VMEM((BLOCK, CHANNELS), BF16),
            pltpu.VMEM((BLOCK, CHANNELS), F32),
            pltpu.VMEM((STATE, CHANNELS), F32),
            pltpu.VMEM((BLOCK, STATE), F32),
            pltpu.VMEM((BLOCK, STATE), F32),
            pltpu.VMEM((BLOCK, CHANNELS), BF16),
            pltpu.VMEM((STATE, LANES), BF16),
            pltpu.VMEM((2, 2, 2, BLOCK, LANES), BF16),
            pltpu.VMEM((2, 2, 2, CORES, X) + tile, BF16),
            pltpu.VMEM((HEADS, TOKENS), F32),
            pltpu.VMEM((HEADS, 8, TOKENS), F32),
            pltpu.VMEM((LANES, LANES), F32),
            pltpu.VMEM((LANES, LANES), F32),
            pltpu.VMEM((BLOCK, STATE, CHANNELS), F32),
            pltpu.VMEM((GROUP, 2, 8, LANES), F32),
            pltpu.VMEM((GROUP, 2, 8, LANES), F32),
            pltpu.VMEM((RESP - 1, STATE, LANES), BF16),
            pltpu.VMEM((2, 8, LANES), F32),
            pltpu.VMEM((X, 2, 8, LANES), F32),
            pltpu.VMEM((GROUP, 8, LANES), F32),
            pltpu.VMEM((GROUP, 8, LANES), F32),
            pltpu.VMEM((STATE, LANES), F32),
            pltpu.VMEM((RESP - 1, STATE, LANES), F32),
            pltpu.VMEM((2, 2, 2, CORES, X) + tile, BF16),
            pltpu.VMEM((2, 2, 2, X) + tile, BF16),
            pltpu.VMEM((2, 4, X) + tile, BF16),
            pltpu.VMEM((2, 2, 3, 4) + half, BF16),
            pltpu.VMEM((2, 2, 4) + half, BF16),
            pltpu.VMEM((2, 2, 3) + half, BF16),
            pltpu.VMEM((2,) + tile, BF16),
            pltpu.VMEM((Z, BLOCK, LANES), BF16),
            pltpu.VMEM((BLOCK, LANES), F32),
            pltpu.VMEM((2 * Y, BLOCK, LANES), F32),
            pltpu.VMEM(wide, BF16),
            pltpu.SemaphoreType.DMA((13,)),
            pltpu.SemaphoreType.DMA((KV_HEADS,)),
            pltpu.SemaphoreType.DMA((SEMS,)),
            pltpu.SemaphoreType.DMA((SEMS,)),
        ],
        compiler_params=pltpu.CompilerParams(
            collective_id=0, has_side_effects=True, vmem_limit_bytes=56 * 2**20
        ),
        name="whole",
    )(
        advantages, lengths, queries, attention_output, grad_out, jnp.swapaxes(own_log_sum_exp, 1, 2), prompt_keys,
        prompt_value_rows, mamba_in, step_size, decay_rate, input_map, output_map, mamba_grad, state_grad,
    )
    return pl.pallas_call(
        finish_kernel,
        out_shape=results,
        in_specs=[anywhere] * 5,
        out_specs=(anywhere,) * 5,
        scratch_shapes=[pltpu.VMEM(r.shape, r.dtype) for r in results]
        + [pltpu.SemaphoreType.DMA((12,)), pltpu.SemaphoreType.DMA((12,))],
        compiler_params=pltpu.CompilerParams(vmem_limit_bytes=60 * 2**20),
        name="finish",
    )(*computed)


def solution(mesh):
    placed = (
        P("resp", "ctx", None),
        P("resp", "ctx", None),
        P("resp", "ctx", None),
        P("resp", "ctx", None),
        P("ctx", None),
        P("ctx", None),
        P("resp"),
        P("resp"),
        P("ctx", "resp"),
        P("ctx", "resp"),
        P(None, "resp"),
        P("ctx", None),
        P("ctx", None),
        P("ctx", "resp"),
        P("resp", None, None),
    )
    return jax.shard_map(
        on_device,
        mesh=mesh,
        in_specs=placed,
        out_specs=(
            P("resp", "ctx", None),
            P("ctx", None),
            P("ctx", None),
            P("ctx", "resp"),
            P("ctx", None),
        ),
        check_vma=False,
    )
```

```python
import functools
import math

import jax
import jax.numpy as jnp
from jax import lax
from jax.experimental import pallas as pl
from jax.experimental.pallas import tpu as pltpu
from jax.sharding import PartitionSpec as P

X, Y, Z, ZH, ZL, CORES, RESP = 4, 4, 16, 4, 4, 2, 16
GROUP = ZH * CORES
HEADS, KV_HEADS, SIZE = 32, 4, 128
PER_KV = HEADS // KV_HEADS
TOKENS = 128
KEYS = 512
BLOCK = 16
STATE = 16
LANES = 128
CHANNELS = 512
SCALE = 1.0 / math.sqrt(SIZE)
LOG2E = math.log2(math.e)
F32 = jnp.float32
BF16 = jnp.bfloat16
MESH = pl.DeviceIdType.MESH
NT = (((1,), (1,)), ((), ()))
VMEM = pl.BlockSpec(memory_space=pltpu.VMEM)


def place():
    ctx = lax.axis_index("ctx")
    resp = lax.axis_index("resp")
    x = lax.div(ctx, GROUP)
    q = lax.rem(ctx, GROUP)
    zh = lax.div(q, CORES)
    c = lax.rem(q, CORES)
    zl = lax.div(resp, Y)
    y = lax.rem(resp, Y)
    return ctx, resp, x, q, zh, c, zl, y


def step(value, offset, count):
    return lax.rem(value + offset + count, count)


LINE, AY, AX, CORE, STATES, TILES, MAPS, BACKS, SUMS = 0, 3, 4, 5, 8, 9, 10, 11, 12
BX, BY, HALVES = 13, 22, 25
FIRST, SECOND, LINES, PIECES = 29, 33, 37, 39
SEMS = 41


def kernel(
    advantages, lengths, queries_h, outputs_h, grads_h, own_h, keys_h, values_h, mamba_in_h, step_h, rate_h,
    input_map_h, output_map_h, mamba_grad_h, state_h,
    query_grad, key_grad, value_grad, mamba_out, map_out,
    queries, outputs, grads, own, keys, values, mamba_in, step_size, decay_rate, input_map, output_map, mamba_grad,
    state_own, blocks, kv, own_t, inners, square, square_in, decays, tiles_out, tiles_in, state_in,
    group_out, group_in, back_out, back_in, db_out, db_in,
    partial, core_in, pairs, first_in, firsts, second_in, lines, line_in, piece, pieces, query_out,
    load_sem, store_sem, send_sem, recv_sem,
):
    ctx, resp, x, q, zh, c, zl, y = place()
    other = 1 - c
    yk, yg = lax.div(y, 2), lax.rem(y, 2)
    z = zh * ZL + zl

    xs = [(step(x, d, X) * GROUP + q, resp) for d in range(1, X)]
    ys = [(ctx, zl * Y + step(y, d, Y)) for d in range(1, Y)]
    zs = [(x * GROUP + step(zh, d, ZH) * CORES + c, resp) for d in range(1, ZH)]
    partner = (x * GROUP + zh * CORES + other, resp)

    def group(d):
        return (x * GROUP + step(q, d, GROUP), resp)

    def resps(d):
        return (ctx, step(resp, d, RESP))

    def each(count, act):
        def one(d, carry):
            act(d)
            return carry

        lax.fori_loop(1, count, one, 0)

    mine = pl.multiple_of(resp * CHANNELS + zh * LANES, LANES)
    loads = [
        (keys_h, keys), (values_h, values), (step_h, step_size), (rate_h, decay_rate), (output_map_h, output_map),
        (mamba_grad_h, mamba_grad), (grads_h, grads), (outputs_h, outputs), (own_h, own), (queries_h, queries),
        (mamba_in_h, mamba_in), (input_map_h, input_map), (state_h.at[0, :, pl.ds(mine, LANES)], state_own),
    ]
    loads = [pltpu.make_async_copy(src, dst, load_sem.at[i]) for i, (src, dst) in enumerate(loads)]
    for load in loads:
        load.start()
    wide = PER_KV * SIZE

    def store(g):
        cols = pl.ds(pl.multiple_of(g * wide, wide), wide)
        return pltpu.make_async_copy(query_out.at[0, :, cols], query_grad.at[0, :, cols], store_sem.at[g])

    barrier = pltpu.get_barrier_semaphore()

    def greet(target):
        pl.semaphore_signal(barrier, inc=1, device_id=target, device_id_type=MESH)

    for target in xs:
        greet(target)
    each(GROUP, lambda d: greet(group(d)))
    each(RESP, lambda d: greet(resps(d)))
    for j in range(1, ZL):
        each(ZH, lambda d: greet((x * GROUP + step(zh, d, ZH) * CORES + c, step(zl, j, ZL) * Y + y)))
    partners = 3 + 7 + 15 + 9

    def send(src, dst, target, sem, recv=None):
        pltpu.make_async_remote_copy(
            src_ref=src, dst_ref=dst, send_sem=send_sem.at[sem], recv_sem=recv_sem.at[sem if recv is None else recv],
            device_id=target, device_id_type=MESH,
        ).start()

    def arrived(ref, sem):
        pltpu.make_async_remote_copy(
            src_ref=ref, dst_ref=ref, send_sem=send_sem.at[sem], recv_sem=recv_sem.at[sem],
            device_id=partner, device_id_type=MESH,
        ).wait_recv()

    def left(ref, sem):
        pltpu.make_async_remote_copy(
            src_ref=ref, dst_ref=ref, send_sem=send_sem.at[sem], recv_sem=recv_sem.at[sem],
            device_id=partner, device_id_type=MESH,
        ).wait_send()

    loads[0].wait()
    loads[1].wait()
    for ch in range(2):
        for kind in range(2):
            for gl in range(2):
                g = ch * 2 + gl
                blocks[ch, kind, gl] = (keys, values)[kind][:, g * LANES:(g + 1) * LANES]
    kv[0, :, :, c, x, zh] = blocks[0]
    kv[1, yk, yg, c, x, zh] = blocks[1, yk, yg]
    pl.semaphore_wait(barrier, partners)
    for gl in range(2):
        for d in range(1, ZH):
            send(blocks.at[0, :, gl], kv.at[0, :, gl, c, x, zh], zs[d - 1], LINE + gl)
    for d in range(1, ZH):
        send(blocks.at[1, yk, yg], kv.at[1, yk, yg, c, x, zh], zs[d - 1], LINE + 2)

    for i in range(2, 6):
        loads[i].wait()
    square[...] = jnp.zeros_like(square)
    square[0:16, 0:16] = output_map[...]
    out_t = square[...].T
    rate = decay_rate[...]
    steps = step_size[...]
    dy = mamba_grad[...].astype(F32)
    carry = jnp.zeros((STATE, CHANNELS), F32)
    for t in range(BLOCK - 1, -1, -1):
        decay = jnp.exp(-steps[t:t + 1] * rate)
        decays[t] = decay
        carry = decay * (out_t[0:STATE, t:t + 1] * dy[t:t + 1] + carry)
    span = jnp.exp(-jnp.sum(steps, axis=0, keepdims=True) * rate)
    for k in range(GROUP):
        kt, nh = k // 2, k % 2
        tiles_out[k, 0] = carry[nh * 8:nh * 8 + 8, kt * LANES:(kt + 1) * LANES]
        tiles_out[k, 1] = span[nh * 8:nh * 8 + 8, kt * LANES:(kt + 1) * LANES]
    each(GROUP, lambda d: send(tiles_out.at[step(q, d, GROUP)], tiles_in.at[q], group(d), TILES))
    tiles_in[q] = tiles_out[q]

    for gl in range(2):
        arrived(kv.at[0, :, gl, c, x, 0:3], LINE + gl)
        here = kv.at[0, :, gl, c, x]
        for d in range(1, 4):
            send(here, here, xs[d - 1], BX + 3 * gl, BX + 3 * gl + d - 1)
        send(here, here, partner, CORE + gl)
    arrived(kv.at[1, yk, yg, c, x, 0:3], LINE + 2)
    for d in range(1, 4):
        here = kv.at[1, yk, yg, c, x, 0:2]
        send(here, here, ys[d - 1], AY)
        here = kv.at[1, yk, yg, c, x, 2:4]
        send(here, here, xs[d - 1], AX)

    def send_state(d):
        start = pl.multiple_of(step(resp, d, RESP) * CHANNELS + zh * LANES, LANES)
        send(state_h.at[0, :, pl.ds(start, LANES)], state_in.at[d - 1], resps(d), STATES)

    each(RESP, send_state)

    length = lengths[0]
    weight = advantages[0] * F32(TOKENS * lax.axis_size("ctx")) / length.astype(F32)
    position = ctx * TOKENS + lax.broadcasted_iota(jnp.int32, (TOKENS, 1), 0)
    token_weight = jnp.where(position < length, weight, F32(0.0))
    ones = jnp.ones((8, SIZE), BF16)

    def prepare(quad, carry):
        for i in range(4):
            h = quad * 4 + i
            cols = pl.ds(pl.multiple_of(h * SIZE, SIZE), SIZE)
            scaled = (grads[0, :, cols].astype(F32) * token_weight).astype(BF16)
            grads[0, :, cols] = scaled
            product = scaled.astype(F32) * outputs[0, :, cols].astype(F32)
            high = product.astype(BF16)
            low = (product - high.astype(F32)).astype(BF16)
            inners[h] = (
                lax.dot_general(ones, high, NT, preferred_element_type=F32)
                + lax.dot_general(ones, low, NT, preferred_element_type=F32)
            )
        return carry

    for i in range(6, 9):
        loads[i].wait()
    own_t[...] = own[0] * LOG2E
    lax.fori_loop(0, 6, prepare, 0)

    arrived(tiles_in.at[0:7], TILES)
    span_all = jnp.ones((8, LANES), F32)
    carry_all = jnp.zeros((8, LANES), F32)
    for k in range(GROUP - 1, -1, -1):
        carry_all = tiles_in[k, 1] * carry_all + tiles_in[k, 0]
        span_all = span_all * tiles_in[k, 1]
    group_out[0] = carry_all
    group_out[1] = span_all
    for d in range(1, X):
        send(group_out, group_in.at[x], xs[d - 1], MAPS)
    group_in[x] = group_out[...]

    def second_gather():
        by_x = kv.at[1, :, :, c, x, 0:2]
        by_y = kv.at[1, yk, yg, c, :, 2:4]
        arrived(kv.at[1, 0, 0, c, 0:3, 0:2], AY)
        arrived(kv.at[1, 0, 0, c, 0:3, 2:4], AX)
        for d in range(1, 4):
            send(by_x, by_x, xs[d - 1], BX + 6, BX + 6 + d - 1)
            send(by_y, by_y, ys[d - 1], BY, BY + d - 1)
        send(by_x, by_x, partner, CORE + 2)
        send(by_y, by_y, partner, CORE + 2)

    def pass_head(gl):
        for d in range(1, 4):
            here = kv.at[0, :, gl, c, step(x, -d, X)]
            arrived(here, BX + 3 * gl + d - 1)
            send(here, here, partner, CORE + gl)

    def pass_chunk():
        for d in range(1, 4):
            here = kv.at[1, :, :, c, step(x, -d, X), 0:2]
            arrived(here, BX + 6 + d - 1)
            send(here, here, partner, CORE + 2)
            from_y = step(y, -d, Y)
            here = kv.at[1, lax.div(from_y, 2), lax.rem(from_y, 2), c, :, 2:4]
            arrived(here, BY + d - 1)
            send(here, here, partner, CORE + 2)

    def carry_back():
        for i in range(10, 13):
            loads[i].wait()
        arrived(state_in.at[0:15], STATES)
        arrived(group_in.at[0:3], MAPS)
        final = state_own[...].astype(F32) + jnp.sum(state_in[...].astype(F32), axis=0)
        incoming = jnp.where(c == 0, final[0:8], final[8:16])
        for k in range(X - 1, 0, -1):
            passed = group_in[k, 1] * incoming + group_in[k, 0]
            incoming = jnp.where(x < k, passed, incoming)
        for k in range(GROUP - 1, -1, -1):
            back_out[k] = incoming
            incoming = tiles_in[k, 1] * incoming + tiles_in[k, 0]
        each(GROUP, lambda d: send(back_out.at[step(q, d, GROUP)], back_in.at[q], group(d), BACKS))
        back_in[q] = back_out[q]

    def rows(ref, pair):
        heads = (2 * pair, 2 * pair + 1)
        return jnp.concatenate([ref[0, :, h * SIZE:(h + 1) * SIZE] for h in heads], axis=0)

    def keys_of(g):
        return kv[g // 2, 0, g % 2].reshape(KEYS, SIZE)

    def begin(pair):
        g = pair // 4
        values_g = kv[g // 2, 1, g % 2].reshape(KEYS, SIZE)
        scores = lax.dot_general(keys_of(g), rows(queries, pair), NT, preferred_element_type=F32) * (SCALE * LOG2E)
        dprobs = lax.dot_general(values_g, rows(grads, pair), NT, preferred_element_type=F32)
        return scores, dprobs

    def end(pair, begun, transposed, sums):
        scores, dprobs = begun
        h = 2 * pair
        inner = jnp.concatenate([inners[h, 0:1], inners[h + 1, 0:1]], axis=1)
        own2 = jnp.concatenate([own_t[h:h + 1], own_t[h + 1:h + 2]], axis=1)
        top = jnp.maximum(jnp.max(scores, axis=0, keepdims=True), own2)
        powers = jnp.exp2(scores - top)
        total = jnp.sum(powers, axis=0, keepdims=True) + jnp.exp2(own2 - top)
        tiled = (KEYS // BLOCK, BLOCK, 2 * SIZE)
        share = jnp.broadcast_to(1.0 / total, (BLOCK, 2 * SIZE)).astype(BF16)
        probs = powers.astype(BF16).reshape(tiled) * share[None]
        dscores = (probs * (dprobs - inner).astype(BF16).reshape(tiled)).reshape(KEYS, 2 * SIZE)
        probs = probs.reshape(KEYS, 2 * SIZE)
        query_t = jnp.dot(transposed, dscores, preferred_element_type=F32) * SCALE
        for i in range(2):
            part = query_t[:, i * SIZE:(i + 1) * SIZE].T.astype(BF16)
            query_out[0, :, (h + i) * SIZE:(h + i + 1) * SIZE] = part
        return (
            sums[0] + jnp.dot(dscores, rows(queries, pair), preferred_element_type=F32),
            sums[1] + jnp.dot(probs, rows(grads, pair), preferred_element_type=F32),
        )

    def ship(g, sums):
        ch, gl = g // 2, g % 2
        for kind in range(2):
            partial[ch, kind, gl] = sums[kind].astype(BF16).reshape(partial.shape[3:])
        send(partial.at[ch, :, gl, other], core_in.at[ch, :, gl], partner, HALVES + g)
        store(g).start()

    def join(g):
        ch, gl = g // 2, g % 2
        arrived(core_in.at[ch, :, gl], HALVES + g)
        for kind in range(2):
            pairs[ch, kind * 2 + gl] = (
                partial[ch, kind, gl, c].astype(F32) + core_in[ch, kind, gl].astype(F32)
            ).astype(BF16)

    def first_hop(ch):
        for d in range(1, 4):
            send(pairs.at[ch, :, step(x, d, X), 0:2], first_in.at[ch, 0, d - 1], xs[d - 1], FIRST + 2 * ch)
            send(pairs.at[ch, step(y, d, Y), :, 2:4], first_in.at[ch, 1, d - 1], ys[d - 1], FIRST + 2 * ch + 1)

    def second_hop(ch):
        for axis in range(2):
            arrived(first_in.at[ch, axis], FIRST + 2 * ch + axis)
            held = pairs[ch, :, x, 0:2] if axis == 0 else pairs[ch, y, :, 2:4]
            total = held.astype(F32)
            for d in range(3):
                total = total + first_in[ch, axis, d].astype(F32)
            firsts[ch, axis] = total.astype(BF16)
            for d in range(1, 4):
                to = step(y, d, Y) if axis == 0 else step(x, d, X)
                target = (ys if axis == 0 else xs)[d - 1]
                send(firsts.at[ch, axis, to], second_in.at[ch, axis, d - 1], target, SECOND + 2 * ch + axis)

    def to_lines(ch):
        for axis in range(2):
            arrived(second_in.at[ch, axis], SECOND + 2 * ch + axis)
            total = firsts[ch, axis, y if axis == 0 else x].astype(F32)
            for d in range(3):
                total = total + second_in[ch, axis, d].astype(F32)
            lines[ch, 2 * axis:2 * axis + 2] = total.astype(BF16)
        for i in range(1, ZH):
            to = step(zh, i, ZH)
            send(lines.at[ch, to], line_in.at[z], (x * GROUP + to * CORES + c, (1 + ch) * Y + y), LINES + ch)

        @pl.when(zl != 1 + ch)
        def _():
            send(lines.at[ch, zh], line_in.at[z], (ctx, (1 + ch) * Y + y), LINES + ch)

    def sum_line(ch):
        @pl.when(zl == 1 + ch)
        def _():
            line_in[z] = lines[ch, zh]
            arrived(line_in.at[0:15], LINES + ch)
            summed = jnp.sum(line_in[...].astype(F32), axis=0).astype(BF16)
            piece[...] = summed
            each(RESP, lambda d: send(piece, pieces.at[ch * Y + y], resps(d), PIECES + ch))
            pieces[ch * Y + y] = summed

    loads[9].wait()
    pass_head(0)
    second_gather()
    lax.fori_loop(6, 8, prepare, 0)
    pass_head(1)
    arrived(kv.at[0, :, 0, other], CORE)
    begun = begin(0)
    for pair in range(HEADS // 2):
        g = pair // 4
        if pair % 4 == 0:
            transposed = keys_of(g).T
            sums = (jnp.zeros((KEYS, SIZE), F32),) * 2
        if pair == 3:
            arrived(kv.at[0, :, 1, other], CORE + 1)
        if pair == 4:
            pass_chunk()
        if pair == 7:
            arrived(kv.at[1, :, :, other], CORE + 2)
        ahead = begin(pair + 1) if pair + 1 < HEADS // 2 else None
        sums = end(pair, begun, transposed, sums)
        begun = ahead
        if pair % 4 == 3:
            ship(g, sums)
            if g == 1:
                join(0)
                carry_back()
            if g == 2:
                join(1)
                first_hop(0)
    join(2)
    second_hop(0)
    join(3)
    first_hop(1)
    to_lines(0)

    arrived(back_in.at[0:7], BACKS)
    square_in[...] = jnp.zeros_like(square_in)
    square_in[0:16, 0:16] = input_map[...]
    in_t = square_in[...].T
    taken = steps * mamba_in[...].astype(F32)
    carry = jnp.concatenate(
        [jnp.concatenate([back_in[kt * 2 + nh] for kt in range(4)], axis=1) for nh in range(2)], axis=0
    )
    lane = lax.broadcasted_iota(jnp.int32, (STATE, LANES), 1)
    db = jnp.zeros((STATE, LANES), F32)
    for t in range(BLOCK - 1, -1, -1):
        adjoint = out_t[0:STATE, t:t + 1] * dy[t:t + 1] + carry
        total = jnp.sum(in_t[0:STATE, t:t + 1] * adjoint, axis=0, keepdims=True)
        mamba_out[t:t + 1, :] = steps[t:t + 1] * total
        term = adjoint * taken[t:t + 1]
        term = (term[:, 0:128] + term[:, 128:256]) + (term[:, 256:384] + term[:, 384:512])
        db = jnp.where(lane == t, jnp.sum(term, axis=1, keepdims=True), db)
        carry = decays[t] * adjoint
    db_out[...] = db

    second_hop(1)
    each(RESP, lambda d: send(db_out, db_in.at[d - 1], resps(d), SUMS))
    to_lines(1)
    sum_line(0)
    sum_line(1)
    arrived(db_in.at[0:15], SUMS)
    square[0:STATE, :] = db_out[...] + jnp.sum(db_in[...], axis=0)
    map_out[...] = square[...].T[0:16, 0:16]

    for gl in range(2):
        left(kv.at[0, :, gl, c, x, 0:3], LINE + gl)
        left(kv.at[0, :, gl, c, 0:3], BX + 3 * gl)
        left(kv.at[0, :, gl, c], CORE + gl)
    left(kv.at[1, 0, 0, c, x, 0:3], LINE + 2)
    left(tiles_out.at[0:7], TILES)
    left(kv.at[1, 0, 0, c, 0:3, 0:2], AY)
    left(kv.at[1, 0, 0, c, 0:3, 2:4], AX)
    left(kv.at[1, :, :, c, 0:3, 0:2], BX + 6)
    left(kv.at[0, :, 0, c, 0:3], BY)
    left(kv.at[1, :, :, c], CORE + 2)
    left(state_in.at[0:15], STATES)
    left(group_in.at[0:3], MAPS)
    left(back_out.at[0:7], BACKS)
    for g in range(KV_HEADS):
        left(core_in.at[g // 2, :, g % 2], HALVES + g)
    for ch in range(2):
        for axis in range(2):
            left(first_in.at[ch, axis], FIRST + 2 * ch + axis)
            left(second_in.at[ch, axis], SECOND + 2 * ch + axis)
    left(db_in.at[0:15], SUMS)
    for ch in range(2):

        @pl.when(zl == 1 + ch)
        def _():
            left(line_in.at[0:3], LINES + ch)
            left(line_in.at[0:15], PIECES + ch)

        @pl.when(zl != 1 + ch)
        def _():
            left(line_in.at[0:4], LINES + ch)

    for g in range(KV_HEADS):
        store(g).wait()

    for ch in range(2):

        @pl.when(zl == 1 + ch)
        def _():
            arrived(pieces.at[0:3], PIECES + ch)

        @pl.when(zl != 1 + ch)
        def _():
            arrived(pieces.at[0:4], PIECES + ch)

        for gl in range(2):
            cols = slice((ch * 2 + gl) * LANES, (ch * 2 + gl + 1) * LANES)
            key_grad[:, cols] = pieces[ch * Y + gl].astype(F32) * SCALE
            value_grad[:, cols] = pieces[ch * Y + 2 + gl].astype(F32)


def finish_kernel(*refs):
    given, results, held = refs[0:5], refs[5:10], refs[10:15]
    sem_in, sem_out = refs[15], refs[16]
    part = (given[0].at[0], held[0].at[0], results[0].at[0])
    moves = [(given[i], held[i], results[i]) for i in range(1, 5)]
    for i in range(8):
        rows = slice(i * BLOCK, (i + 1) * BLOCK)
        moves.append(tuple(ref.at[rows] for ref in part))
    copies_in = [pltpu.make_async_copy(src, mid, sem_in.at[i]) for i, (src, mid, _) in enumerate(moves)]
    copies_out = [pltpu.make_async_copy(mid, dst, sem_out.at[i]) for i, (_, mid, dst) in enumerate(moves)]
    for copy in copies_in:
        copy.start()
    for first, then in zip(copies_in, copies_out):
        first.wait()
        then.start()
    for copy in copies_out:
        copy.wait()


def on_device(
    queries, attention_output, grad_out, own_log_sum_exp, prompt_keys, prompt_value_rows, advantages, lengths,
    mamba_in, step_size, decay_rate, input_map, output_map, mamba_grad, state_grad,
):
    smem = pl.BlockSpec(memory_space=pltpu.SMEM)
    anywhere = pl.BlockSpec(memory_space=pl.ANY)
    tile = (ZH, BLOCK, LANES)
    half = (2, BLOCK, LANES)
    wide = (1, TOKENS, HEADS * SIZE)
    block_grad = jax.ShapeDtypeStruct((BLOCK, KV_HEADS * SIZE), F32)
    results = (
        jax.ShapeDtypeStruct(wide, BF16),
        block_grad,
        block_grad,
        jax.ShapeDtypeStruct((BLOCK, CHANNELS), F32),
        jax.ShapeDtypeStruct((BLOCK, STATE), F32),
    )
    computed = pl.pallas_call(
        kernel,
        out_shape=results,
        in_specs=[smem] * 2 + [anywhere] * 13,
        out_specs=(anywhere,) + (VMEM,) * 4,
        scratch_shapes=[
            pltpu.VMEM(wide, BF16),
            pltpu.VMEM(wide, BF16),
            pltpu.VMEM(wide, BF16),
            pltpu.VMEM((1, HEADS, TOKENS), F32),
            pltpu.VMEM((BLOCK, KV_HEADS * SIZE), BF16),
            pltpu.VMEM((BLOCK, KV_HEADS * SIZE), BF16),
            pltpu.VMEM((BLOCK, CHANNELS), BF16),
            pltpu.VMEM((BLOCK, CHANNELS), F32),
            pltpu.VMEM((STATE, CHANNELS), F32),
            pltpu.VMEM((BLOCK, STATE), F32),
            pltpu.VMEM((BLOCK, STATE), F32),
            pltpu.VMEM((BLOCK, CHANNELS), BF16),
            pltpu.VMEM((STATE, LANES), BF16),
            pltpu.VMEM((2, 2, 2, BLOCK, LANES), BF16),
            pltpu.VMEM((2, 2, 2, CORES, X) + tile, BF16),
            pltpu.VMEM((HEADS, TOKENS), F32),
            pltpu.VMEM((HEADS, 8, TOKENS), F32),
            pltpu.VMEM((LANES, LANES), F32),
            pltpu.VMEM((LANES, LANES), F32),
            pltpu.VMEM((BLOCK, STATE, CHANNELS), F32),
            pltpu.VMEM((GROUP, 2, 8, LANES), F32),
            pltpu.VMEM((GROUP, 2, 8, LANES), F32),
            pltpu.VMEM((RESP - 1, STATE, LANES), BF16),
            pltpu.VMEM((2, 8, LANES), F32),
            pltpu.VMEM((X, 2, 8, LANES), F32),
            pltpu.VMEM((GROUP, 8, LANES), F32),
            pltpu.VMEM((GROUP, 8, LANES), F32),
            pltpu.VMEM((STATE, LANES), F32),
            pltpu.VMEM((RESP - 1, STATE, LANES), F32),
            pltpu.VMEM((2, 2, 2, CORES, X) + tile, BF16),
            pltpu.VMEM((2, 2, 2, X) + tile, BF16),
            pltpu.VMEM((2, 4, X) + tile, BF16),
            pltpu.VMEM((2, 2, 3, 4) + half, BF16),
            pltpu.VMEM((2, 2, 4) + half, BF16),
            pltpu.VMEM((2, 2, 3) + half, BF16),
            pltpu.VMEM((2,) + tile, BF16),
            pltpu.VMEM((Z, BLOCK, LANES), BF16),
            pltpu.VMEM((BLOCK, LANES), BF16),
            pltpu.VMEM((2 * Y, BLOCK, LANES), BF16),
            pltpu.VMEM(wide, BF16),
            pltpu.SemaphoreType.DMA((13,)),
            pltpu.SemaphoreType.DMA((KV_HEADS,)),
            pltpu.SemaphoreType.DMA((SEMS,)),
            pltpu.SemaphoreType.DMA((SEMS,)),
        ],
        compiler_params=pltpu.CompilerParams(
            collective_id=0, has_side_effects=True, vmem_limit_bytes=56 * 2**20
        ),
        name="whole",
    )(
        advantages, lengths, queries, attention_output, grad_out, jnp.swapaxes(own_log_sum_exp, 1, 2), prompt_keys,
        prompt_value_rows, mamba_in, step_size, decay_rate, input_map, output_map, mamba_grad, state_grad,
    )
    return pl.pallas_call(
        finish_kernel,
        out_shape=results,
        in_specs=[anywhere] * 5,
        out_specs=(anywhere,) * 5,
        scratch_shapes=[pltpu.VMEM(r.shape, r.dtype) for r in results]
        + [pltpu.SemaphoreType.DMA((12,)), pltpu.SemaphoreType.DMA((12,))],
        compiler_params=pltpu.CompilerParams(vmem_limit_bytes=60 * 2**20),
        name="finish",
    )(*computed)


def solution(mesh):
    placed = (
        P("resp", "ctx", None),
        P("resp", "ctx", None),
        P("resp", "ctx", None),
        P("resp", "ctx", None),
        P("ctx", None),
        P("ctx", None),
        P("resp"),
        P("resp"),
        P("ctx", "resp"),
        P("ctx", "resp"),
        P(None, "resp"),
        P("ctx", None),
        P("ctx", None),
        P("ctx", "resp"),
        P("resp", None, None),
    )
    return jax.shard_map(
        on_device,
        mesh=mesh,
        in_specs=placed,
        out_specs=(
            P("resp", "ctx", None),
            P("ctx", None),
            P("ctx", None),
            P("ctx", "resp"),
            P("ctx", None),
        ),
        check_vma=False,
    )
```

```python
import functools
import math

import jax
import jax.numpy as jnp
from jax import lax
from jax.experimental import pallas as pl
from jax.experimental.pallas import tpu as pltpu
from jax.sharding import PartitionSpec as P

X, Y, Z, ZH, ZL, CORES, RESP = 4, 4, 16, 4, 4, 2, 16
GROUP = ZH * CORES
HEADS, KV_HEADS, SIZE = 32, 4, 128
PER_KV = HEADS // KV_HEADS
TOKENS = 128
KEYS = 512
BLOCK = 16
STATE = 16
LANES = 128
CHANNELS = 512
SCALE = 1.0 / math.sqrt(SIZE)
LOG2E = math.log2(math.e)
F32 = jnp.float32
BF16 = jnp.bfloat16
MESH = pl.DeviceIdType.MESH
NT = (((1,), (1,)), ((), ()))
VMEM = pl.BlockSpec(memory_space=pltpu.VMEM)


def place():
    ctx = lax.axis_index("ctx")
    resp = lax.axis_index("resp")
    x = lax.div(ctx, GROUP)
    q = lax.rem(ctx, GROUP)
    zh = lax.div(q, CORES)
    c = lax.rem(q, CORES)
    zl = lax.div(resp, Y)
    y = lax.rem(resp, Y)
    return ctx, resp, x, q, zh, c, zl, y


def step(value, offset, count):
    return lax.rem(value + offset + count, count)


LINE, AY, AX, CORE, STATES, TILES, MAPS, BACKS, SUMS = 0, 3, 4, 5, 8, 9, 10, 11, 12
BX, BY, HALVES = 13, 22, 25
FIRST, SECOND, LINES, PIECES = 29, 33, 37, 39
SEMS = 41


def kernel(
    advantages, lengths, queries_h, outputs_h, grads_h, own_h, keys_h, values_h, mamba_in_h, step_h, rate_h,
    input_map_h, output_map_h, mamba_grad_h, state_h,
    query_grad, key_grad, value_grad, mamba_out, map_out,
    queries, outputs, grads, own, keys, values, mamba_in, step_size, decay_rate, input_map, output_map, mamba_grad,
    state_own, blocks, kv, own_t, inners, square, square_in, decays, tiles_out, tiles_in, state_in,
    group_out, group_in, back_out, back_in, db_out, db_in,
    partial, core_in, pairs, first_in, firsts, second_in, lines, line_in, piece, pieces, query_out,
    load_sem, store_sem, send_sem, recv_sem,
):
    ctx, resp, x, q, zh, c, zl, y = place()
    other = 1 - c
    yk, yg = lax.div(y, 2), lax.rem(y, 2)
    z = zh * ZL + zl

    xs = [(step(x, d, X) * GROUP + q, resp) for d in range(1, X)]
    ys = [(ctx, zl * Y + step(y, d, Y)) for d in range(1, Y)]
    zs = [(x * GROUP + step(zh, d, ZH) * CORES + c, resp) for d in range(1, ZH)]
    partner = (x * GROUP + zh * CORES + other, resp)

    def group(d):
        return (x * GROUP + step(q, d, GROUP), resp)

    def resps(d):
        return (ctx, step(resp, d, RESP))

    def each(count, act):
        def one(d, carry):
            act(d)
            return carry

        lax.fori_loop(1, count, one, 0)

    mine = pl.multiple_of(resp * CHANNELS + zh * LANES, LANES)
    loads = [
        (keys_h, keys), (values_h, values), (step_h, step_size), (rate_h, decay_rate), (output_map_h, output_map),
        (mamba_grad_h, mamba_grad), (grads_h, grads), (outputs_h, outputs), (own_h, own), (queries_h, queries),
        (mamba_in_h, mamba_in), (input_map_h, input_map), (state_h.at[0, :, pl.ds(mine, LANES)], state_own),
    ]
    loads = [pltpu.make_async_copy(src, dst, load_sem.at[i]) for i, (src, dst) in enumerate(loads)]
    for load in loads:
        load.start()
    wide = PER_KV * SIZE

    def store(g):
        cols = pl.ds(pl.multiple_of(g * wide, wide), wide)
        return pltpu.make_async_copy(query_out.at[0, :, cols], query_grad.at[0, :, cols], store_sem.at[g])

    barrier = pltpu.get_barrier_semaphore()

    def greet(target):
        pl.semaphore_signal(barrier, inc=1, device_id=target, device_id_type=MESH)

    for target in xs:
        greet(target)
    each(GROUP, lambda d: greet(group(d)))
    each(RESP, lambda d: greet(resps(d)))
    for j in range(1, ZL):
        each(ZH, lambda d: greet((x * GROUP + step(zh, d, ZH) * CORES + c, step(zl, j, ZL) * Y + y)))
    partners = 3 + 7 + 15 + 9

    def send(src, dst, target, sem, recv=None):
        pltpu.make_async_remote_copy(
            src_ref=src, dst_ref=dst, send_sem=send_sem.at[sem], recv_sem=recv_sem.at[sem if recv is None else recv],
            device_id=target, device_id_type=MESH,
        ).start()

    def arrived(ref, sem):
        pltpu.make_async_remote_copy(
            src_ref=ref, dst_ref=ref, send_sem=send_sem.at[sem], recv_sem=recv_sem.at[sem],
            device_id=partner, device_id_type=MESH,
        ).wait_recv()

    def left(ref, sem):
        pltpu.make_async_remote_copy(
            src_ref=ref, dst_ref=ref, send_sem=send_sem.at[sem], recv_sem=recv_sem.at[sem],
            device_id=partner, device_id_type=MESH,
        ).wait_send()

    loads[0].wait()
    loads[1].wait()
    for ch in range(2):
        for kind in range(2):
            for gl in range(2):
                g = ch * 2 + gl
                blocks[ch, kind, gl] = (keys, values)[kind][:, g * LANES:(g + 1) * LANES]
    kv[0, :, :, c, x, zh] = blocks[0]
    kv[1, yk, yg, c, x, zh] = blocks[1, yk, yg]
    pl.semaphore_wait(barrier, partners)
    for gl in range(2):
        for d in range(1, ZH):
            send(blocks.at[0, :, gl], kv.at[0, :, gl, c, x, zh], zs[d - 1], LINE + gl)
    for d in range(1, ZH):
        send(blocks.at[1, yk, yg], kv.at[1, yk, yg, c, x, zh], zs[d - 1], LINE + 2)

    for i in range(2, 6):
        loads[i].wait()
    square[...] = jnp.zeros_like(square)
    square[0:16, 0:16] = output_map[...]
    out_t = square[...].T
    rate = decay_rate[...]
    steps = step_size[...]
    dy = mamba_grad[...].astype(F32)
    carry = jnp.zeros((STATE, CHANNELS), F32)
    for t in range(BLOCK - 1, -1, -1):
        decay = jnp.exp(-steps[t:t + 1] * rate)
        decays[t] = decay
        carry = decay * (out_t[0:STATE, t:t + 1] * dy[t:t + 1] + carry)
    span = jnp.exp(-jnp.sum(steps, axis=0, keepdims=True) * rate)
    for k in range(GROUP):
        kt, nh = k // 2, k % 2
        tiles_out[k, 0] = carry[nh * 8:nh * 8 + 8, kt * LANES:(kt + 1) * LANES]
        tiles_out[k, 1] = span[nh * 8:nh * 8 + 8, kt * LANES:(kt + 1) * LANES]
    each(GROUP, lambda d: send(tiles_out.at[step(q, d, GROUP)], tiles_in.at[q], group(d), TILES))
    tiles_in[q] = tiles_out[q]

    for gl in range(2):
        arrived(kv.at[0, :, gl, c, x, 0:3], LINE + gl)
        here = kv.at[0, :, gl, c, x]
        for d in range(1, 4):
            send(here, here, xs[d - 1], BX + 3 * gl, BX + 3 * gl + d - 1)
        send(here, here, partner, CORE + gl)
    arrived(kv.at[1, yk, yg, c, x, 0:3], LINE + 2)
    for d in range(1, 4):
        here = kv.at[1, yk, yg, c, x, 0:2]
        send(here, here, ys[d - 1], AY)
        here = kv.at[1, yk, yg, c, x, 2:4]
        send(here, here, xs[d - 1], AX)

    def send_state(d):
        start = pl.multiple_of(step(resp, d, RESP) * CHANNELS + zh * LANES, LANES)
        send(state_h.at[0, :, pl.ds(start, LANES)], state_in.at[d - 1], resps(d), STATES)

    each(RESP, send_state)

    length = lengths[0]
    weight = advantages[0] * F32(TOKENS * lax.axis_size("ctx")) / length.astype(F32)
    position = ctx * TOKENS + lax.broadcasted_iota(jnp.int32, (TOKENS, 1), 0)
    token_weight = jnp.where(position < length, weight, F32(0.0))
    ones = jnp.ones((8, SIZE), BF16)

    def prepare(quad, carry):
        for i in range(4):
            h = quad * 4 + i
            cols = pl.ds(pl.multiple_of(h * SIZE, SIZE), SIZE)
            scaled = (grads[0, :, cols].astype(F32) * token_weight).astype(BF16)
            grads[0, :, cols] = scaled
            product = scaled.astype(F32) * outputs[0, :, cols].astype(F32)
            high = product.astype(BF16)
            low = (product - high.astype(F32)).astype(BF16)
            inners[h] = (
                lax.dot_general(ones, high, NT, preferred_element_type=F32)
                + lax.dot_general(ones, low, NT, preferred_element_type=F32)
            )
        return carry

    for i in range(6, 9):
        loads[i].wait()
    own_t[...] = own[0] * LOG2E
    lax.fori_loop(0, 6, prepare, 0)

    arrived(tiles_in.at[0:7], TILES)
    span_all = jnp.ones((8, LANES), F32)
    carry_all = jnp.zeros((8, LANES), F32)
    for k in range(GROUP - 1, -1, -1):
        carry_all = tiles_in[k, 1] * carry_all + tiles_in[k, 0]
        span_all = span_all * tiles_in[k, 1]
    group_out[0] = carry_all
    group_out[1] = span_all
    for d in range(1, X):
        send(group_out, group_in.at[x], xs[d - 1], MAPS)
    group_in[x] = group_out[...]

    def second_gather():
        by_x = kv.at[1, :, :, c, x, 0:2]
        by_y = kv.at[1, yk, yg, c, :, 2:4]
        arrived(kv.at[1, 0, 0, c, 0:3, 0:2], AY)
        arrived(kv.at[1, 0, 0, c, 0:3, 2:4], AX)
        for d in range(1, 4):
            send(by_x, by_x, xs[d - 1], BX + 6, BX + 6 + d - 1)
            send(by_y, by_y, ys[d - 1], BY, BY + d - 1)
        send(by_x, by_x, partner, CORE + 2)
        send(by_y, by_y, partner, CORE + 2)

    def pass_head(gl):
        for d in range(1, 4):
            here = kv.at[0, :, gl, c, step(x, -d, X)]
            arrived(here, BX + 3 * gl + d - 1)
            send(here, here, partner, CORE + gl)

    def pass_chunk():
        for d in range(1, 4):
            here = kv.at[1, :, :, c, step(x, -d, X), 0:2]
            arrived(here, BX + 6 + d - 1)
            send(here, here, partner, CORE + 2)
            from_y = step(y, -d, Y)
            here = kv.at[1, lax.div(from_y, 2), lax.rem(from_y, 2), c, :, 2:4]
            arrived(here, BY + d - 1)
            send(here, here, partner, CORE + 2)

    def carry_back():
        for i in range(10, 13):
            loads[i].wait()
        arrived(state_in.at[0:15], STATES)
        arrived(group_in.at[0:3], MAPS)
        final = state_own[...].astype(F32) + jnp.sum(state_in[...].astype(F32), axis=0)
        incoming = jnp.where(c == 0, final[0:8], final[8:16])
        for k in range(X - 1, 0, -1):
            passed = group_in[k, 1] * incoming + group_in[k, 0]
            incoming = jnp.where(x < k, passed, incoming)
        for k in range(GROUP - 1, -1, -1):
            back_out[k] = incoming
            incoming = tiles_in[k, 1] * incoming + tiles_in[k, 0]
        each(GROUP, lambda d: send(back_out.at[step(q, d, GROUP)], back_in.at[q], group(d), BACKS))
        back_in[q] = back_out[q]

    def rows(ref, pair):
        heads = (2 * pair, 2 * pair + 1)
        return jnp.concatenate([ref[0, :, h * SIZE:(h + 1) * SIZE] for h in heads], axis=0)

    def keys_of(g):
        return kv[g // 2, 0, g % 2].reshape(KEYS, SIZE)

    def begin(pair):
        g = pair // 4
        values_g = kv[g // 2, 1, g % 2].reshape(KEYS, SIZE)
        scores = lax.dot_general(keys_of(g), rows(queries, pair), NT, preferred_element_type=F32) * (SCALE * LOG2E)
        dprobs = lax.dot_general(values_g, rows(grads, pair), NT, preferred_element_type=F32)
        return scores, dprobs

    def end(pair, begun, transposed, sums):
        scores, dprobs = begun
        h = 2 * pair
        inner = jnp.concatenate([inners[h, 0:1], inners[h + 1, 0:1]], axis=1)
        own2 = jnp.concatenate([own_t[h:h + 1], own_t[h + 1:h + 2]], axis=1)
        top = jnp.maximum(jnp.max(scores, axis=0, keepdims=True), own2)
        powers = jnp.exp2(scores - top)
        total = jnp.sum(powers, axis=0, keepdims=True) + jnp.exp2(own2 - top)
        probs = powers * (1.0 / total)
        dscores = (probs * (dprobs - inner)).astype(BF16)
        query_t = jnp.dot(transposed, dscores, preferred_element_type=F32) * SCALE
        for i in range(2):
            part = query_t[:, i * SIZE:(i + 1) * SIZE].T.astype(BF16)
            query_out[0, :, (h + i) * SIZE:(h + i + 1) * SIZE] = part
        return (
            sums[0] + jnp.dot(dscores, rows(queries, pair), preferred_element_type=F32),
            sums[1] + jnp.dot(probs.astype(BF16), rows(grads, pair), preferred_element_type=F32),
        )

    def ship(g, sums):
        ch, gl = g // 2, g % 2
        for kind in range(2):
            partial[ch, kind, gl] = sums[kind].astype(BF16).reshape(partial.shape[3:])
        send(partial.at[ch, :, gl, other], core_in.at[ch, :, gl], partner, HALVES + g)
        store(g).start()

    def finish_scan():
        arrived(back_in.at[0:7], BACKS)
        square_in[...] = jnp.zeros_like(square_in)
        square_in[0:16, 0:16] = input_map[...]
        in_t = square_in[...].T
        taken = steps * mamba_in[...].astype(F32)
        carry = jnp.concatenate(
            [jnp.concatenate([back_in[kt * 2 + nh] for kt in range(4)], axis=1) for nh in range(2)], axis=0
        )
        lane = lax.broadcasted_iota(jnp.int32, (STATE, LANES), 1)
        db = jnp.zeros((STATE, LANES), F32)
        for t in range(BLOCK - 1, -1, -1):
            adjoint = out_t[0:STATE, t:t + 1] * dy[t:t + 1] + carry
            total = jnp.sum(in_t[0:STATE, t:t + 1] * adjoint, axis=0, keepdims=True)
            mamba_out[t:t + 1, :] = steps[t:t + 1] * total
            term = adjoint * taken[t:t + 1]
            term = (term[:, 0:128] + term[:, 128:256]) + (term[:, 256:384] + term[:, 384:512])
            db = jnp.where(lane == t, jnp.sum(term, axis=1, keepdims=True), db)
            carry = decays[t] * adjoint
        db_out[...] = db
        each(RESP, lambda d: send(db_out, db_in.at[d - 1], resps(d), SUMS))

    def join(g):
        ch, gl = g // 2, g % 2
        arrived(core_in.at[ch, :, gl], HALVES + g)
        for kind in range(2):
            pairs[ch, kind * 2 + gl] = (
                partial[ch, kind, gl, c].astype(F32) + core_in[ch, kind, gl].astype(F32)
            ).astype(BF16)

    def first_hop(ch):
        for d in range(1, 4):
            send(pairs.at[ch, :, step(x, d, X), 0:2], first_in.at[ch, 0, d - 1], xs[d - 1], FIRST + 2 * ch)
            send(pairs.at[ch, step(y, d, Y), :, 2:4], first_in.at[ch, 1, d - 1], ys[d - 1], FIRST + 2 * ch + 1)

    def second_hop(ch):
        for axis in range(2):
            arrived(first_in.at[ch, axis], FIRST + 2 * ch + axis)
            held = pairs[ch, :, x, 0:2] if axis == 0 else pairs[ch, y, :, 2:4]
            total = held.astype(F32)
            for d in range(3):
                total = total + first_in[ch, axis, d].astype(F32)
            firsts[ch, axis] = total.astype(BF16)
            for d in range(1, 4):
                to = step(y, d, Y) if axis == 0 else step(x, d, X)
                target = (ys if axis == 0 else xs)[d - 1]
                send(firsts.at[ch, axis, to], second_in.at[ch, axis, d - 1], target, SECOND + 2 * ch + axis)

    def to_lines(ch):
        for axis in range(2):
            arrived(second_in.at[ch, axis], SECOND + 2 * ch + axis)
            total = firsts[ch, axis, y if axis == 0 else x].astype(F32)
            for d in range(3):
                total = total + second_in[ch, axis, d].astype(F32)
            lines[ch, 2 * axis:2 * axis + 2] = total.astype(BF16)
        for i in range(1, ZH):
            to = step(zh, i, ZH)
            send(lines.at[ch, to], line_in.at[z], (x * GROUP + to * CORES + c, (1 + ch) * Y + y), LINES + ch)

        @pl.when(zl != 1 + ch)
        def _():
            send(lines.at[ch, zh], line_in.at[z], (ctx, (1 + ch) * Y + y), LINES + ch)

    def sum_line(ch):
        @pl.when(zl == 1 + ch)
        def _():
            line_in[z] = lines[ch, zh]
            arrived(line_in.at[0:15], LINES + ch)
            summed = jnp.sum(line_in[...].astype(F32), axis=0).astype(BF16)
            piece[...] = summed
            each(RESP, lambda d: send(piece, pieces.at[ch * Y + y], resps(d), PIECES + ch))
            pieces[ch * Y + y] = summed

    loads[9].wait()
    pass_head(0)
    second_gather()
    lax.fori_loop(6, 8, prepare, 0)
    pass_head(1)
    arrived(kv.at[0, :, 0, other], CORE)
    begun = begin(0)
    for pair in range(HEADS // 2):
        g = pair // 4
        if pair % 4 == 0:
            transposed = keys_of(g).T
            sums = (jnp.zeros((KEYS, SIZE), F32),) * 2
        if pair == 3:
            arrived(kv.at[0, :, 1, other], CORE + 1)
        if pair == 4:
            pass_chunk()
        if pair == 7:
            arrived(kv.at[1, :, :, other], CORE + 2)
        ahead = begin(pair + 1) if pair + 1 < HEADS // 2 else None
        sums = end(pair, begun, transposed, sums)
        begun = ahead
        if pair % 4 == 3:
            ship(g, sums)
            if g == 1:
                join(0)
                carry_back()
            if g == 2:
                join(1)
                first_hop(0)
                finish_scan()
    join(2)
    second_hop(0)
    join(3)
    first_hop(1)
    to_lines(0)

    second_hop(1)
    to_lines(1)
    sum_line(0)
    sum_line(1)
    arrived(db_in.at[0:15], SUMS)
    square[0:STATE, :] = db_out[...] + jnp.sum(db_in[...], axis=0)
    map_out[...] = square[...].T[0:16, 0:16]

    for gl in range(2):
        left(kv.at[0, :, gl, c, x, 0:3], LINE + gl)
        left(kv.at[0, :, gl, c, 0:3], BX + 3 * gl)
        left(kv.at[0, :, gl, c], CORE + gl)
    left(kv.at[1, 0, 0, c, x, 0:3], LINE + 2)
    left(tiles_out.at[0:7], TILES)
    left(kv.at[1, 0, 0, c, 0:3, 0:2], AY)
    left(kv.at[1, 0, 0, c, 0:3, 2:4], AX)
    left(kv.at[1, :, :, c, 0:3, 0:2], BX + 6)
    left(kv.at[0, :, 0, c, 0:3], BY)
    left(kv.at[1, :, :, c], CORE + 2)
    left(state_in.at[0:15], STATES)
    left(group_in.at[0:3], MAPS)
    left(back_out.at[0:7], BACKS)
    for g in range(KV_HEADS):
        left(core_in.at[g // 2, :, g % 2], HALVES + g)
    for ch in range(2):
        for axis in range(2):
            left(first_in.at[ch, axis], FIRST + 2 * ch + axis)
            left(second_in.at[ch, axis], SECOND + 2 * ch + axis)
    left(db_in.at[0:15], SUMS)
    for ch in range(2):

        @pl.when(zl == 1 + ch)
        def _():
            left(line_in.at[0:3], LINES + ch)
            left(line_in.at[0:15], PIECES + ch)

        @pl.when(zl != 1 + ch)
        def _():
            left(line_in.at[0:4], LINES + ch)

    for g in range(KV_HEADS):
        store(g).wait()

    for ch in range(2):

        @pl.when(zl == 1 + ch)
        def _():
            arrived(pieces.at[0:3], PIECES + ch)

        @pl.when(zl != 1 + ch)
        def _():
            arrived(pieces.at[0:4], PIECES + ch)

        for gl in range(2):
            cols = slice((ch * 2 + gl) * LANES, (ch * 2 + gl + 1) * LANES)
            key_grad[:, cols] = pieces[ch * Y + gl].astype(F32) * SCALE
            value_grad[:, cols] = pieces[ch * Y + 2 + gl].astype(F32)


def finish_kernel(*refs):
    given, results, held = refs[0:5], refs[5:10], refs[10:15]
    sem_in, sem_out = refs[15], refs[16]
    part = (given[0].at[0], held[0].at[0], results[0].at[0])
    moves = [(given[i], held[i], results[i]) for i in range(1, 5)]
    for i in range(8):
        rows = slice(i * BLOCK, (i + 1) * BLOCK)
        moves.append(tuple(ref.at[rows] for ref in part))
    copies_in = [pltpu.make_async_copy(src, mid, sem_in.at[i]) for i, (src, mid, _) in enumerate(moves)]
    copies_out = [pltpu.make_async_copy(mid, dst, sem_out.at[i]) for i, (_, mid, dst) in enumerate(moves)]
    for copy in copies_in:
        copy.start()
    for first, then in zip(copies_in, copies_out):
        first.wait()
        then.start()
    for copy in copies_out:
        copy.wait()


def on_device(
    queries, attention_output, grad_out, own_log_sum_exp, prompt_keys, prompt_value_rows, advantages, lengths,
    mamba_in, step_size, decay_rate, input_map, output_map, mamba_grad, state_grad,
):
    smem = pl.BlockSpec(memory_space=pltpu.SMEM)
    anywhere = pl.BlockSpec(memory_space=pl.ANY)
    tile = (ZH, BLOCK, LANES)
    half = (2, BLOCK, LANES)
    wide = (1, TOKENS, HEADS * SIZE)
    block_grad = jax.ShapeDtypeStruct((BLOCK, KV_HEADS * SIZE), F32)
    results = (
        jax.ShapeDtypeStruct(wide, BF16),
        block_grad,
        block_grad,
        jax.ShapeDtypeStruct((BLOCK, CHANNELS), F32),
        jax.ShapeDtypeStruct((BLOCK, STATE), F32),
    )
    computed = pl.pallas_call(
        kernel,
        out_shape=results,
        in_specs=[smem] * 2 + [anywhere] * 13,
        out_specs=(anywhere,) + (VMEM,) * 4,
        scratch_shapes=[
            pltpu.VMEM(wide, BF16),
            pltpu.VMEM(wide, BF16),
            pltpu.VMEM(wide, BF16),
            pltpu.VMEM((1, HEADS, TOKENS), F32),
            pltpu.VMEM((BLOCK, KV_HEADS * SIZE), BF16),
            pltpu.VMEM((BLOCK, KV_HEADS * SIZE), BF16),
            pltpu.VMEM((BLOCK, CHANNELS), BF16),
            pltpu.VMEM((BLOCK, CHANNELS), F32),
            pltpu.VMEM((STATE, CHANNELS), F32),
            pltpu.VMEM((BLOCK, STATE), F32),
            pltpu.VMEM((BLOCK, STATE), F32),
            pltpu.VMEM((BLOCK, CHANNELS), BF16),
            pltpu.VMEM((STATE, LANES), BF16),
            pltpu.VMEM((2, 2, 2, BLOCK, LANES), BF16),
            pltpu.VMEM((2, 2, 2, CORES, X) + tile, BF16),
            pltpu.VMEM((HEADS, TOKENS), F32),
            pltpu.VMEM((HEADS, 8, TOKENS), F32),
            pltpu.VMEM((LANES, LANES), F32),
            pltpu.VMEM((LANES, LANES), F32),
            pltpu.VMEM((BLOCK, STATE, CHANNELS), F32),
            pltpu.VMEM((GROUP, 2, 8, LANES), F32),
            pltpu.VMEM((GROUP, 2, 8, LANES), F32),
            pltpu.VMEM((RESP - 1, STATE, LANES), BF16),
            pltpu.VMEM((2, 8, LANES), F32),
            pltpu.VMEM((X, 2, 8, LANES), F32),
            pltpu.VMEM((GROUP, 8, LANES), F32),
            pltpu.VMEM((GROUP, 8, LANES), F32),
            pltpu.VMEM((STATE, LANES), F32),
            pltpu.VMEM((RESP - 1, STATE, LANES), F32),
            pltpu.VMEM((2, 2, 2, CORES, X) + tile, BF16),
            pltpu.VMEM((2, 2, 2, X) + tile, BF16),
            pltpu.VMEM((2, 4, X) + tile, BF16),
            pltpu.VMEM((2, 2, 3, 4) + half, BF16),
            pltpu.VMEM((2, 2, 4) + half, BF16),
            pltpu.VMEM((2, 2, 3) + half, BF16),
            pltpu.VMEM((2,) + tile, BF16),
            pltpu.VMEM((Z, BLOCK, LANES), BF16),
            pltpu.VMEM((BLOCK, LANES), BF16),
            pltpu.VMEM((2 * Y, BLOCK, LANES), BF16),
            pltpu.VMEM(wide, BF16),
            pltpu.SemaphoreType.DMA((13,)),
            pltpu.SemaphoreType.DMA((KV_HEADS,)),
            pltpu.SemaphoreType.DMA((SEMS,)),
            pltpu.SemaphoreType.DMA((SEMS,)),
        ],
        compiler_params=pltpu.CompilerParams(
            collective_id=0, has_side_effects=True, vmem_limit_bytes=56 * 2**20
        ),
        name="whole",
    )(
        advantages, lengths, queries, attention_output, grad_out, jnp.swapaxes(own_log_sum_exp, 1, 2), prompt_keys,
        prompt_value_rows, mamba_in, step_size, decay_rate, input_map, output_map, mamba_grad, state_grad,
    )
    return pl.pallas_call(
        finish_kernel,
        out_shape=results,
        in_specs=[anywhere] * 5,
        out_specs=(anywhere,) * 5,
        scratch_shapes=[pltpu.VMEM(r.shape, r.dtype) for r in results]
        + [pltpu.SemaphoreType.DMA((12,)), pltpu.SemaphoreType.DMA((12,))],
        compiler_params=pltpu.CompilerParams(vmem_limit_bytes=60 * 2**20),
        name="finish",
    )(*computed)


def solution(mesh):
    placed = (
        P("resp", "ctx", None),
        P("resp", "ctx", None),
        P("resp", "ctx", None),
        P("resp", "ctx", None),
        P("ctx", None),
        P("ctx", None),
        P("resp"),
        P("resp"),
        P("ctx", "resp"),
        P("ctx", "resp"),
        P(None, "resp"),
        P("ctx", None),
        P("ctx", None),
        P("ctx", "resp"),
        P("resp", None, None),
    )
    return jax.shard_map(
        on_device,
        mesh=mesh,
        in_specs=placed,
        out_specs=(
            P("resp", "ctx", None),
            P("ctx", None),
            P("ctx", None),
            P("ctx", "resp"),
            P("ctx", None),
        ),
        check_vma=False,
    )
```

```python
import functools
import math

import jax
import jax.numpy as jnp
from jax import lax
from jax.experimental import pallas as pl
from jax.experimental.pallas import tpu as pltpu
from jax.sharding import PartitionSpec as P

X, Y, Z, ZH, ZL, CORES, RESP = 4, 4, 16, 4, 4, 2, 16
GROUP = ZH * CORES
HEADS, KV_HEADS, SIZE = 32, 4, 128
PER_KV = HEADS // KV_HEADS
TOKENS = 128
KEYS = 512
BLOCK = 16
STATE = 16
LANES = 128
CHANNELS = 512
SCALE = 1.0 / math.sqrt(SIZE)
LOG2E = math.log2(math.e)
F32 = jnp.float32
BF16 = jnp.bfloat16
MESH = pl.DeviceIdType.MESH
NT = (((1,), (1,)), ((), ()))
VMEM = pl.BlockSpec(memory_space=pltpu.VMEM)


def place():
    ctx = lax.axis_index("ctx")
    resp = lax.axis_index("resp")
    x = lax.div(ctx, GROUP)
    q = lax.rem(ctx, GROUP)
    zh = lax.div(q, CORES)
    c = lax.rem(q, CORES)
    zl = lax.div(resp, Y)
    y = lax.rem(resp, Y)
    return ctx, resp, x, q, zh, c, zl, y


def step(value, offset, count):
    return lax.rem(value + offset + count, count)


LINE, AY, AX, CORE, STATES, TILES, MAPS, BACKS, SUMS = 0, 3, 4, 5, 8, 9, 10, 11, 12
BX, BY, HALVES = 13, 22, 25
FIRST, SECOND, LINES, PIECES = 29, 33, 37, 39
SEMS = 41


def kernel(
    advantages, lengths, queries_h, outputs_h, grads_h, own_h, keys_h, values_h, mamba_in_h, step_h, rate_h,
    input_map_h, output_map_h, mamba_grad_h, state_h,
    query_grad, key_grad, value_grad, mamba_out, map_out,
    queries, outputs, grads, own, keys, values, mamba_in, step_size, decay_rate, input_map, output_map, mamba_grad,
    state_own, blocks, kv, own_t, inners, square, square_in, decays, tiles_out, tiles_in, state_in,
    group_out, group_in, back_out, back_in, db_out, db_in,
    partial, core_in, pairs, first_in, firsts, second_in, lines, line_in, piece, pieces, query_out,
    load_sem, store_sem, send_sem, recv_sem,
):
    ctx, resp, x, q, zh, c, zl, y = place()
    other = 1 - c
    yk, yg = lax.div(y, 2), lax.rem(y, 2)
    z = zh * ZL + zl

    xs = [(step(x, d, X) * GROUP + q, resp) for d in range(1, X)]
    ys = [(ctx, zl * Y + step(y, d, Y)) for d in range(1, Y)]
    zs = [(x * GROUP + step(zh, d, ZH) * CORES + c, resp) for d in range(1, ZH)]
    partner = (x * GROUP + zh * CORES + other, resp)

    def group(d):
        return (x * GROUP + step(q, d, GROUP), resp)

    def resps(d):
        return (ctx, step(resp, d, RESP))

    def each(count, act):
        def one(d, carry):
            act(d)
            return carry

        lax.fori_loop(1, count, one, 0)

    mine = pl.multiple_of(resp * CHANNELS + zh * LANES, LANES)
    loads = [
        (keys_h, keys), (values_h, values), (step_h, step_size), (rate_h, decay_rate), (output_map_h, output_map),
        (mamba_grad_h, mamba_grad), (grads_h, grads), (outputs_h, outputs), (own_h, own), (queries_h, queries),
        (mamba_in_h, mamba_in), (input_map_h, input_map), (state_h.at[0, :, pl.ds(mine, LANES)], state_own),
    ]
    loads = [pltpu.make_async_copy(src, dst, load_sem.at[i]) for i, (src, dst) in enumerate(loads)]
    for load in loads:
        load.start()
    wide = PER_KV * SIZE

    def store(g):
        cols = pl.ds(pl.multiple_of(g * wide, wide), wide)
        return pltpu.make_async_copy(query_out.at[0, :, cols], query_grad.at[0, :, cols], store_sem.at[g])

    barrier = pltpu.get_barrier_semaphore()

    def greet(target):
        pl.semaphore_signal(barrier, inc=1, device_id=target, device_id_type=MESH)

    for target in xs:
        greet(target)
    each(GROUP, lambda d: greet(group(d)))
    each(RESP, lambda d: greet(resps(d)))
    for j in range(1, ZL):
        each(ZH, lambda d: greet((x * GROUP + step(zh, d, ZH) * CORES + c, step(zl, j, ZL) * Y + y)))
    partners = 3 + 7 + 15 + 9

    def send(src, dst, target, sem, recv=None):
        pltpu.make_async_remote_copy(
            src_ref=src, dst_ref=dst, send_sem=send_sem.at[sem], recv_sem=recv_sem.at[sem if recv is None else recv],
            device_id=target, device_id_type=MESH,
        ).start()

    def arrived(ref, sem):
        pltpu.make_async_remote_copy(
            src_ref=ref, dst_ref=ref, send_sem=send_sem.at[sem], recv_sem=recv_sem.at[sem],
            device_id=partner, device_id_type=MESH,
        ).wait_recv()

    def left(ref, sem):
        pltpu.make_async_remote_copy(
            src_ref=ref, dst_ref=ref, send_sem=send_sem.at[sem], recv_sem=recv_sem.at[sem],
            device_id=partner, device_id_type=MESH,
        ).wait_send()

    loads[0].wait()
    loads[1].wait()
    for ch in range(2):
        for kind in range(2):
            for gl in range(2):
                g = ch * 2 + gl
                blocks[ch, kind, gl] = (keys, values)[kind][:, g * LANES:(g + 1) * LANES]
    kv[0, :, :, c, x, zh] = blocks[0]
    kv[1, yk, yg, c, x, zh] = blocks[1, yk, yg]
    pl.semaphore_wait(barrier, partners)
    for gl in range(2):
        for d in range(1, ZH):
            send(blocks.at[0, :, gl], kv.at[0, :, gl, c, x, zh], zs[d - 1], LINE + gl)
    for d in range(1, ZH):
        send(blocks.at[1, yk, yg], kv.at[1, yk, yg, c, x, zh], zs[d - 1], LINE + 2)

    for i in range(2, 6):
        loads[i].wait()
    square[...] = jnp.zeros_like(square)
    square[0:16, 0:16] = output_map[...]
    out_t = square[...].T
    rate = decay_rate[...]
    steps = step_size[...]
    dy = mamba_grad[...].astype(F32)
    carry = jnp.zeros((STATE, CHANNELS), F32)
    for t in range(BLOCK - 1, -1, -1):
        decay = jnp.exp(-steps[t:t + 1] * rate)
        decays[t] = decay
        carry = decay * (out_t[0:STATE, t:t + 1] * dy[t:t + 1] + carry)
    span = jnp.exp(-jnp.sum(steps, axis=0, keepdims=True) * rate)
    for k in range(GROUP):
        kt, nh = k // 2, k % 2
        tiles_out[k, 0] = carry[nh * 8:nh * 8 + 8, kt * LANES:(kt + 1) * LANES]
        tiles_out[k, 1] = span[nh * 8:nh * 8 + 8, kt * LANES:(kt + 1) * LANES]
    each(GROUP, lambda d: send(tiles_out.at[step(q, d, GROUP)], tiles_in.at[q], group(d), TILES))
    tiles_in[q] = tiles_out[q]

    for gl in range(2):
        arrived(kv.at[0, :, gl, c, x, 0:3], LINE + gl)
        here = kv.at[0, :, gl, c, x]
        for d in range(1, 4):
            send(here, here, xs[d - 1], BX + 3 * gl, BX + 3 * gl + d - 1)
        send(here, here, partner, CORE + gl)
    arrived(kv.at[1, yk, yg, c, x, 0:3], LINE + 2)
    for d in range(1, 4):
        here = kv.at[1, yk, yg, c, x, 0:2]
        send(here, here, ys[d - 1], AY)
        here = kv.at[1, yk, yg, c, x, 2:4]
        send(here, here, xs[d - 1], AX)

    def send_state(d):
        start = pl.multiple_of(step(resp, d, RESP) * CHANNELS + zh * LANES, LANES)
        send(state_h.at[0, :, pl.ds(start, LANES)], state_in.at[d - 1], resps(d), STATES)

    each(RESP, send_state)

    length = lengths[0]
    weight = advantages[0] * F32(TOKENS * lax.axis_size("ctx")) / length.astype(F32)
    position = ctx * TOKENS + lax.broadcasted_iota(jnp.int32, (TOKENS, 1), 0)
    token_weight = jnp.where(position < length, weight, F32(0.0))
    ones = jnp.ones((8, 2 * SIZE), BF16)

    def prepare(quad, carry):
        for i in range(2):
            pair = quad * 2 + i
            cols = pl.ds(pl.multiple_of(pair * 2 * SIZE, 2 * SIZE), 2 * SIZE)
            scaled = (grads[0, :, cols].astype(F32) * token_weight).astype(BF16)
            grads[0, :, cols] = scaled
            product = scaled.astype(F32) * outputs[0, :, cols].astype(F32)
            product = jnp.concatenate([product[:, 0:SIZE], product[:, SIZE:2 * SIZE]], axis=0)
            high = product.astype(BF16)
            low = (product - high.astype(F32)).astype(BF16)
            both = jnp.concatenate([high, low], axis=1)
            inners[pair] = lax.dot_general(ones, both, NT, preferred_element_type=F32)
        return carry

    for i in range(6, 9):
        loads[i].wait()
    own_t[...] = own[0] * LOG2E
    lax.fori_loop(0, 6, prepare, 0)

    arrived(tiles_in.at[0:7], TILES)
    span_all = jnp.ones((8, LANES), F32)
    carry_all = jnp.zeros((8, LANES), F32)
    for k in range(GROUP - 1, -1, -1):
        carry_all = tiles_in[k, 1] * carry_all + tiles_in[k, 0]
        span_all = span_all * tiles_in[k, 1]
    group_out[0] = carry_all
    group_out[1] = span_all
    for d in range(1, X):
        send(group_out, group_in.at[x], xs[d - 1], MAPS)
    group_in[x] = group_out[...]

    def second_gather():
        by_x = kv.at[1, :, :, c, x, 0:2]
        by_y = kv.at[1, yk, yg, c, :, 2:4]
        arrived(kv.at[1, 0, 0, c, 0:3, 0:2], AY)
        arrived(kv.at[1, 0, 0, c, 0:3, 2:4], AX)
        for d in range(1, 4):
            send(by_x, by_x, xs[d - 1], BX + 6, BX + 6 + d - 1)
            send(by_y, by_y, ys[d - 1], BY, BY + d - 1)
        send(by_x, by_x, partner, CORE + 2)
        send(by_y, by_y, partner, CORE + 2)

    def pass_head(gl):
        for d in range(1, 4):
            here = kv.at[0, :, gl, c, step(x, -d, X)]
            arrived(here, BX + 3 * gl + d - 1)
            send(here, here, partner, CORE + gl)

    def pass_chunk():
        for d in range(1, 4):
            here = kv.at[1, :, :, c, step(x, -d, X), 0:2]
            arrived(here, BX + 6 + d - 1)
            send(here, here, partner, CORE + 2)
            from_y = step(y, -d, Y)
            here = kv.at[1, lax.div(from_y, 2), lax.rem(from_y, 2), c, :, 2:4]
            arrived(here, BY + d - 1)
            send(here, here, partner, CORE + 2)

    def carry_back():
        for i in range(10, 13):
            loads[i].wait()
        arrived(state_in.at[0:15], STATES)
        arrived(group_in.at[0:3], MAPS)
        final = state_own[...].astype(F32) + jnp.sum(state_in[...].astype(F32), axis=0)
        incoming = jnp.where(c == 0, final[0:8], final[8:16])
        for k in range(X - 1, 0, -1):
            passed = group_in[k, 1] * incoming + group_in[k, 0]
            incoming = jnp.where(x < k, passed, incoming)
        for k in range(GROUP - 1, -1, -1):
            back_out[k] = incoming
            incoming = tiles_in[k, 1] * incoming + tiles_in[k, 0]
        each(GROUP, lambda d: send(back_out.at[step(q, d, GROUP)], back_in.at[q], group(d), BACKS))
        back_in[q] = back_out[q]

    def rows(ref, pair):
        heads = (2 * pair, 2 * pair + 1)
        return jnp.concatenate([ref[0, :, h * SIZE:(h + 1) * SIZE] for h in heads], axis=0)

    def keys_of(g):
        return kv[g // 2, 0, g % 2].reshape(KEYS, SIZE)

    def begin(pair):
        g = pair // 4
        values_g = kv[g // 2, 1, g % 2].reshape(KEYS, SIZE)
        scores = lax.dot_general(keys_of(g), rows(queries, pair), NT, preferred_element_type=F32) * (SCALE * LOG2E)
        dprobs = lax.dot_general(values_g, rows(grads, pair), NT, preferred_element_type=F32)
        return scores, dprobs

    def end(pair, begun, transposed, sums):
        scores, dprobs = begun
        h = 2 * pair
        inner = inners[pair, 0:1]
        own2 = jnp.concatenate([own_t[h:h + 1], own_t[h + 1:h + 2]], axis=1)
        top = jnp.maximum(jnp.max(scores, axis=0, keepdims=True), own2)
        powers = jnp.exp2(scores - top)
        total = jnp.sum(powers, axis=0, keepdims=True) + jnp.exp2(own2 - top)
        probs = powers * (1.0 / total)
        dscores = (probs * (dprobs - inner)).astype(BF16)
        query_t = jnp.dot(transposed, dscores, preferred_element_type=F32) * SCALE
        for i in range(2):
            part = query_t[:, i * SIZE:(i + 1) * SIZE].T.astype(BF16)
            query_out[0, :, (h + i) * SIZE:(h + i + 1) * SIZE] = part
        return (
            sums[0] + jnp.dot(dscores, rows(queries, pair), preferred_element_type=F32),
            sums[1] + jnp.dot(probs.astype(BF16), rows(grads, pair), preferred_element_type=F32),
        )

    def ship(g, sums):
        ch, gl = g // 2, g % 2
        for kind in range(2):
            partial[ch, kind, gl] = sums[kind].astype(BF16).reshape(partial.shape[3:])
        send(partial.at[ch, :, gl, other], core_in.at[ch, :, gl], partner, HALVES + g)
        store(g).start()

    def join(g):
        ch, gl = g // 2, g % 2
        arrived(core_in.at[ch, :, gl], HALVES + g)
        for kind in range(2):
            pairs[ch, kind * 2 + gl] = (
                partial[ch, kind, gl, c].astype(F32) + core_in[ch, kind, gl].astype(F32)
            ).astype(BF16)

    def first_hop(ch):
        for d in range(1, 4):
            send(pairs.at[ch, :, step(x, d, X), 0:2], first_in.at[ch, 0, d - 1], xs[d - 1], FIRST + 2 * ch)
            send(pairs.at[ch, step(y, d, Y), :, 2:4], first_in.at[ch, 1, d - 1], ys[d - 1], FIRST + 2 * ch + 1)

    def second_hop(ch):
        for axis in range(2):
            arrived(first_in.at[ch, axis], FIRST + 2 * ch + axis)
            held = pairs[ch, :, x, 0:2] if axis == 0 else pairs[ch, y, :, 2:4]
            total = held.astype(F32)
            for d in range(3):
                total = total + first_in[ch, axis, d].astype(F32)
            firsts[ch, axis] = total.astype(BF16)
            for d in range(1, 4):
                to = step(y, d, Y) if axis == 0 else step(x, d, X)
                target = (ys if axis == 0 else xs)[d - 1]
                send(firsts.at[ch, axis, to], second_in.at[ch, axis, d - 1], target, SECOND + 2 * ch + axis)

    def to_lines(ch):
        for axis in range(2):
            arrived(second_in.at[ch, axis], SECOND + 2 * ch + axis)
            total = firsts[ch, axis, y if axis == 0 else x].astype(F32)
            for d in range(3):
                total = total + second_in[ch, axis, d].astype(F32)
            lines[ch, 2 * axis:2 * axis + 2] = total.astype(BF16)
        for i in range(1, ZH):
            to = step(zh, i, ZH)
            send(lines.at[ch, to], line_in.at[z], (x * GROUP + to * CORES + c, (1 + ch) * Y + y), LINES + ch)

        @pl.when(zl != 1 + ch)
        def _():
            send(lines.at[ch, zh], line_in.at[z], (ctx, (1 + ch) * Y + y), LINES + ch)

    def sum_line(ch):
        @pl.when(zl == 1 + ch)
        def _():
            line_in[z] = lines[ch, zh]
            arrived(line_in.at[0:15], LINES + ch)
            summed = jnp.sum(line_in[...].astype(F32), axis=0).astype(BF16)
            piece[...] = summed
            each(RESP, lambda d: send(piece, pieces.at[ch * Y + y], resps(d), PIECES + ch))
            pieces[ch * Y + y] = summed

    loads[9].wait()
    pass_head(0)
    second_gather()
    lax.fori_loop(6, 8, prepare, 0)
    pass_head(1)
    carry_back()
    arrived(kv.at[0, :, 0, other], CORE)
    begun = begin(0)
    for pair in range(HEADS // 2):
        g = pair // 4
        if pair % 4 == 0:
            transposed = keys_of(g).T
            sums = (jnp.zeros((KEYS, SIZE), F32),) * 2
        if pair == 3:
            arrived(kv.at[0, :, 1, other], CORE + 1)
        if pair == 4:
            pass_chunk()
        if pair == 7:
            arrived(kv.at[1, :, :, other], CORE + 2)
        ahead = begin(pair + 1) if pair + 1 < HEADS // 2 else None
        sums = end(pair, begun, transposed, sums)
        begun = ahead
        if pair % 4 == 3:
            ship(g, sums)
            if g == 1:
                join(0)
            if g == 2:
                join(1)
                first_hop(0)
    join(2)
    second_hop(0)
    join(3)
    first_hop(1)
    to_lines(0)

    arrived(back_in.at[0:7], BACKS)
    square_in[...] = jnp.zeros_like(square_in)
    square_in[0:16, 0:16] = input_map[...]
    in_t = square_in[...].T
    taken = steps * mamba_in[...].astype(F32)
    carry = jnp.concatenate(
        [jnp.concatenate([back_in[kt * 2 + nh] for kt in range(4)], axis=1) for nh in range(2)], axis=0
    )
    lane = lax.broadcasted_iota(jnp.int32, (STATE, LANES), 1)
    db = jnp.zeros((STATE, LANES), F32)
    for t in range(BLOCK - 1, -1, -1):
        adjoint = out_t[0:STATE, t:t + 1] * dy[t:t + 1] + carry
        total = jnp.sum(in_t[0:STATE, t:t + 1] * adjoint, axis=0, keepdims=True)
        mamba_out[t:t + 1, :] = steps[t:t + 1] * total
        term = adjoint * taken[t:t + 1]
        term = (term[:, 0:128] + term[:, 128:256]) + (term[:, 256:384] + term[:, 384:512])
        db = jnp.where(lane == t, jnp.sum(term, axis=1, keepdims=True), db)
        carry = decays[t] * adjoint
    db_out[...] = db

    second_hop(1)
    each(RESP, lambda d: send(db_out, db_in.at[d - 1], resps(d), SUMS))
    to_lines(1)
    sum_line(0)
    sum_line(1)
    arrived(db_in.at[0:15], SUMS)
    square[0:STATE, :] = db_out[...] + jnp.sum(db_in[...], axis=0)
    map_out[...] = square[...].T[0:16, 0:16]

    for gl in range(2):
        left(kv.at[0, :, gl, c, x, 0:3], LINE + gl)
        left(kv.at[0, :, gl, c, 0:3], BX + 3 * gl)
        left(kv.at[0, :, gl, c], CORE + gl)
    left(kv.at[1, 0, 0, c, x, 0:3], LINE + 2)
    left(tiles_out.at[0:7], TILES)
    left(kv.at[1, 0, 0, c, 0:3, 0:2], AY)
    left(kv.at[1, 0, 0, c, 0:3, 2:4], AX)
    left(kv.at[1, :, :, c, 0:3, 0:2], BX + 6)
    left(kv.at[0, :, 0, c, 0:3], BY)
    left(kv.at[1, :, :, c], CORE + 2)
    left(state_in.at[0:15], STATES)
    left(group_in.at[0:3], MAPS)
    left(back_out.at[0:7], BACKS)
    for g in range(KV_HEADS):
        left(core_in.at[g // 2, :, g % 2], HALVES + g)
    for ch in range(2):
        for axis in range(2):
            left(first_in.at[ch, axis], FIRST + 2 * ch + axis)
            left(second_in.at[ch, axis], SECOND + 2 * ch + axis)
    left(db_in.at[0:15], SUMS)
    for ch in range(2):

        @pl.when(zl == 1 + ch)
        def _():
            left(line_in.at[0:3], LINES + ch)
            left(line_in.at[0:15], PIECES + ch)

        @pl.when(zl != 1 + ch)
        def _():
            left(line_in.at[0:4], LINES + ch)

    for g in range(KV_HEADS):
        store(g).wait()

    for ch in range(2):

        @pl.when(zl == 1 + ch)
        def _():
            arrived(pieces.at[0:3], PIECES + ch)

        @pl.when(zl != 1 + ch)
        def _():
            arrived(pieces.at[0:4], PIECES + ch)

        for gl in range(2):
            cols = slice((ch * 2 + gl) * LANES, (ch * 2 + gl + 1) * LANES)
            key_grad[:, cols] = pieces[ch * Y + gl].astype(F32) * SCALE
            value_grad[:, cols] = pieces[ch * Y + 2 + gl].astype(F32)


def finish_kernel(*refs):
    given, results, held = refs[0:5], refs[5:10], refs[10:15]
    sem_in, sem_out = refs[15], refs[16]
    part = (given[0].at[0], held[0].at[0], results[0].at[0])
    moves = [(given[i], held[i], results[i]) for i in range(1, 5)]
    for i in range(8):
        rows = slice(i * BLOCK, (i + 1) * BLOCK)
        moves.append(tuple(ref.at[rows] for ref in part))
    copies_in = [pltpu.make_async_copy(src, mid, sem_in.at[i]) for i, (src, mid, _) in enumerate(moves)]
    copies_out = [pltpu.make_async_copy(mid, dst, sem_out.at[i]) for i, (_, mid, dst) in enumerate(moves)]
    for copy in copies_in:
        copy.start()
    for first, then in zip(copies_in, copies_out):
        first.wait()
        then.start()
    for copy in copies_out:
        copy.wait()


def on_device(
    queries, attention_output, grad_out, own_log_sum_exp, prompt_keys, prompt_value_rows, advantages, lengths,
    mamba_in, step_size, decay_rate, input_map, output_map, mamba_grad, state_grad,
):
    smem = pl.BlockSpec(memory_space=pltpu.SMEM)
    anywhere = pl.BlockSpec(memory_space=pl.ANY)
    tile = (ZH, BLOCK, LANES)
    half = (2, BLOCK, LANES)
    wide = (1, TOKENS, HEADS * SIZE)
    block_grad = jax.ShapeDtypeStruct((BLOCK, KV_HEADS * SIZE), F32)
    results = (
        jax.ShapeDtypeStruct(wide, BF16),
        block_grad,
        block_grad,
        jax.ShapeDtypeStruct((BLOCK, CHANNELS), F32),
        jax.ShapeDtypeStruct((BLOCK, STATE), F32),
    )
    computed = pl.pallas_call(
        kernel,
        out_shape=results,
        in_specs=[smem] * 2 + [anywhere] * 13,
        out_specs=(anywhere,) + (VMEM,) * 4,
        scratch_shapes=[
            pltpu.VMEM(wide, BF16),
            pltpu.VMEM(wide, BF16),
            pltpu.VMEM(wide, BF16),
            pltpu.VMEM((1, HEADS, TOKENS), F32),
            pltpu.VMEM((BLOCK, KV_HEADS * SIZE), BF16),
            pltpu.VMEM((BLOCK, KV_HEADS * SIZE), BF16),
            pltpu.VMEM((BLOCK, CHANNELS), BF16),
            pltpu.VMEM((BLOCK, CHANNELS), F32),
            pltpu.VMEM((STATE, CHANNELS), F32),
            pltpu.VMEM((BLOCK, STATE), F32),
            pltpu.VMEM((BLOCK, STATE), F32),
            pltpu.VMEM((BLOCK, CHANNELS), BF16),
            pltpu.VMEM((STATE, LANES), BF16),
            pltpu.VMEM((2, 2, 2, BLOCK, LANES), BF16),
            pltpu.VMEM((2, 2, 2, CORES, X) + tile, BF16),
            pltpu.VMEM((HEADS, TOKENS), F32),
            pltpu.VMEM((HEADS // 2, 8, 2 * TOKENS), F32),
            pltpu.VMEM((LANES, LANES), F32),
            pltpu.VMEM((LANES, LANES), F32),
            pltpu.VMEM((BLOCK, STATE, CHANNELS), F32),
            pltpu.VMEM((GROUP, 2, 8, LANES), F32),
            pltpu.VMEM((GROUP, 2, 8, LANES), F32),
            pltpu.VMEM((RESP - 1, STATE, LANES), BF16),
            pltpu.VMEM((2, 8, LANES), F32),
            pltpu.VMEM((X, 2, 8, LANES), F32),
            pltpu.VMEM((GROUP, 8, LANES), F32),
            pltpu.VMEM((GROUP, 8, LANES), F32),
            pltpu.VMEM((STATE, LANES), F32),
            pltpu.VMEM((RESP - 1, STATE, LANES), F32),
            pltpu.VMEM((2, 2, 2, CORES, X) + tile, BF16),
            pltpu.VMEM((2, 2, 2, X) + tile, BF16),
            pltpu.VMEM((2, 4, X) + tile, BF16),
            pltpu.VMEM((2, 2, 3, 4) + half, BF16),
            pltpu.VMEM((2, 2, 4) + half, BF16),
            pltpu.VMEM((2, 2, 3) + half, BF16),
            pltpu.VMEM((2,) + tile, BF16),
            pltpu.VMEM((Z, BLOCK, LANES), BF16),
            pltpu.VMEM((BLOCK, LANES), BF16),
            pltpu.VMEM((2 * Y, BLOCK, LANES), BF16),
            pltpu.VMEM(wide, BF16),
            pltpu.SemaphoreType.DMA((13,)),
            pltpu.SemaphoreType.DMA((KV_HEADS,)),
            pltpu.SemaphoreType.DMA((SEMS,)),
            pltpu.SemaphoreType.DMA((SEMS,)),
        ],
        compiler_params=pltpu.CompilerParams(
            collective_id=0, has_side_effects=True, vmem_limit_bytes=56 * 2**20
        ),
        name="whole",
    )(
        advantages, lengths, queries, attention_output, grad_out, jnp.swapaxes(own_log_sum_exp, 1, 2), prompt_keys,
        prompt_value_rows, mamba_in, step_size, decay_rate, input_map, output_map, mamba_grad, state_grad,
    )
    return pl.pallas_call(
        finish_kernel,
        out_shape=results,
        in_specs=[anywhere] * 5,
        out_specs=(anywhere,) * 5,
        scratch_shapes=[pltpu.VMEM(r.shape, r.dtype) for r in results]
        + [pltpu.SemaphoreType.DMA((12,)), pltpu.SemaphoreType.DMA((12,))],
        compiler_params=pltpu.CompilerParams(vmem_limit_bytes=60 * 2**20),
        name="finish",
    )(*computed)


def solution(mesh):
    placed = (
        P("resp", "ctx", None),
        P("resp", "ctx", None),
        P("resp", "ctx", None),
        P("resp", "ctx", None),
        P("ctx", None),
        P("ctx", None),
        P("resp"),
        P("resp"),
        P("ctx", "resp"),
        P("ctx", "resp"),
        P(None, "resp"),
        P("ctx", None),
        P("ctx", None),
        P("ctx", "resp"),
        P("resp", None, None),
    )
    return jax.shard_map(
        on_device,
        mesh=mesh,
        in_specs=placed,
        out_specs=(
            P("resp", "ctx", None),
            P("ctx", None),
            P("ctx", None),
            P("ctx", "resp"),
            P("ctx", None),
        ),
        check_vma=False,
    )
```

```python
import functools
import math

import jax
import jax.numpy as jnp
from jax import lax
from jax.experimental import pallas as pl
from jax.experimental.pallas import tpu as pltpu
from jax.sharding import PartitionSpec as P

X, Y, Z, ZH, ZL, CORES, RESP = 4, 4, 16, 4, 4, 2, 16
GROUP = ZH * CORES
HEADS, KV_HEADS, SIZE = 32, 4, 128
PER_KV = HEADS // KV_HEADS
TOKENS = 128
KEYS = 512
BLOCK = 16
STATE = 16
LANES = 128
CHANNELS = 512
SCALE = 1.0 / math.sqrt(SIZE)
LOG2E = math.log2(math.e)
F32 = jnp.float32
BF16 = jnp.bfloat16
MESH = pl.DeviceIdType.MESH
NT = (((1,), (1,)), ((), ()))
VMEM = pl.BlockSpec(memory_space=pltpu.VMEM)


def place():
    ctx = lax.axis_index("ctx")
    resp = lax.axis_index("resp")
    x = lax.div(ctx, GROUP)
    q = lax.rem(ctx, GROUP)
    zh = lax.div(q, CORES)
    c = lax.rem(q, CORES)
    zl = lax.div(resp, Y)
    y = lax.rem(resp, Y)
    return ctx, resp, x, q, zh, c, zl, y


def step(value, offset, count):
    return lax.rem(value + offset + count, count)


FAR_FIRST, FAR_LAST = (2, 1, 3), (1, 3, 2)
LINE, AY, AX, CORE, STATES, TILES, MAPS, BACKS, SUMS = 0, 3, 4, 5, 8, 9, 10, 11, 12
BX, BY, HALVES = 13, 22, 25
FIRST, SECOND, LINES, PIECES = 29, 33, 37, 39
SEMS = 41


def kernel(
    advantages, lengths, queries_h, outputs_h, grads_h, own_h, keys_h, values_h, mamba_in_h, step_h, rate_h,
    input_map_h, output_map_h, mamba_grad_h, state_h,
    query_grad, key_grad, value_grad, mamba_out, map_out,
    queries, outputs, grads, own, keys, values, mamba_in, step_size, decay_rate, input_map, output_map, mamba_grad,
    state_own, blocks, kv, own_t, inners, square, square_in, decays, tiles_out, tiles_in, state_in,
    group_out, group_in, back_out, back_in, db_out, db_in,
    partial, core_in, pairs, first_in, firsts, second_in, lines, line_in, piece, pieces, query_out,
    load_sem, store_sem, send_sem, recv_sem,
):
    ctx, resp, x, q, zh, c, zl, y = place()
    other = 1 - c
    yk, yg = lax.div(y, 2), lax.rem(y, 2)
    z = zh * ZL + zl

    xs = [(step(x, d, X) * GROUP + q, resp) for d in range(1, X)]
    ys = [(ctx, zl * Y + step(y, d, Y)) for d in range(1, Y)]
    zs = [(x * GROUP + step(zh, d, ZH) * CORES + c, resp) for d in range(1, ZH)]
    partner = (x * GROUP + zh * CORES + other, resp)

    def group(d):
        return (x * GROUP + step(q, d, GROUP), resp)

    def resps(d):
        return (ctx, step(resp, d, RESP))

    def each(count, act):
        def one(d, carry):
            act(d)
            return carry

        lax.fori_loop(1, count, one, 0)

    mine = pl.multiple_of(resp * CHANNELS + zh * LANES, LANES)
    loads = [
        (keys_h, keys), (values_h, values), (step_h, step_size), (rate_h, decay_rate), (output_map_h, output_map),
        (mamba_grad_h, mamba_grad), (grads_h, grads), (outputs_h, outputs), (own_h, own), (queries_h, queries),
        (mamba_in_h, mamba_in), (input_map_h, input_map), (state_h.at[0, :, pl.ds(mine, LANES)], state_own),
    ]
    loads = [pltpu.make_async_copy(src, dst, load_sem.at[i]) for i, (src, dst) in enumerate(loads)]
    for load in loads[0:2]:
        load.start()
    wide = PER_KV * SIZE

    def store(g):
        cols = pl.ds(pl.multiple_of(g * wide, wide), wide)
        return pltpu.make_async_copy(query_out.at[0, :, cols], query_grad.at[0, :, cols], store_sem.at[g])

    barrier = pltpu.get_barrier_semaphore()

    def greet(target):
        pl.semaphore_signal(barrier, inc=1, device_id=target, device_id_type=MESH)

    for target in xs:
        greet(target)
    each(GROUP, lambda d: greet(group(d)))
    each(RESP, lambda d: greet(resps(d)))
    for j in range(1, ZL):
        each(ZH, lambda d: greet((x * GROUP + step(zh, d, ZH) * CORES + c, step(zl, j, ZL) * Y + y)))
    partners = 3 + 7 + 15 + 9
    for load in loads[2:]:
        load.start()

    def send(src, dst, target, sem, recv=None):
        pltpu.make_async_remote_copy(
            src_ref=src, dst_ref=dst, send_sem=send_sem.at[sem], recv_sem=recv_sem.at[sem if recv is None else recv],
            device_id=target, device_id_type=MESH,
        ).start()

    def arrived(ref, sem):
        pltpu.make_async_remote_copy(
            src_ref=ref, dst_ref=ref, send_sem=send_sem.at[sem], recv_sem=recv_sem.at[sem],
            device_id=partner, device_id_type=MESH,
        ).wait_recv()

    def left(ref, sem):
        pltpu.make_async_remote_copy(
            src_ref=ref, dst_ref=ref, send_sem=send_sem.at[sem], recv_sem=recv_sem.at[sem],
            device_id=partner, device_id_type=MESH,
        ).wait_send()

    loads[0].wait()
    loads[1].wait()
    for ch in range(2):
        for kind in range(2):
            for gl in range(2):
                g = ch * 2 + gl
                blocks[ch, kind, gl] = (keys, values)[kind][:, g * LANES:(g + 1) * LANES]
    kv[0, :, :, c, x, zh] = blocks[0]
    kv[1, yk, yg, c, x, zh] = blocks[1, yk, yg]
    pl.semaphore_wait(barrier, partners)
    for gl in range(2):
        for d in FAR_FIRST:
            send(blocks.at[0, :, gl], kv.at[0, :, gl, c, x, zh], zs[d - 1], LINE + gl)
    for d in FAR_FIRST:
        send(blocks.at[1, yk, yg], kv.at[1, yk, yg, c, x, zh], zs[d - 1], LINE + 2)

    for i in range(2, 6):
        loads[i].wait()
    square[...] = jnp.zeros_like(square)
    square[0:16, 0:16] = output_map[...]
    out_t = square[...].T
    rate = decay_rate[...]
    steps = step_size[...]
    dy = mamba_grad[...].astype(F32)
    carry = jnp.zeros((STATE, CHANNELS), F32)
    for t in range(BLOCK - 1, -1, -1):
        decay = jnp.exp(-steps[t:t + 1] * rate)
        decays[t] = decay
        carry = decay * (out_t[0:STATE, t:t + 1] * dy[t:t + 1] + carry)
    span = jnp.exp(-jnp.sum(steps, axis=0, keepdims=True) * rate)
    for k in range(GROUP):
        kt, nh = k // 2, k % 2
        tiles_out[k, 0] = carry[nh * 8:nh * 8 + 8, kt * LANES:(kt + 1) * LANES]
        tiles_out[k, 1] = span[nh * 8:nh * 8 + 8, kt * LANES:(kt + 1) * LANES]
    each(GROUP, lambda d: send(tiles_out.at[step(q, d, GROUP)], tiles_in.at[q], group(d), TILES))
    tiles_in[q] = tiles_out[q]

    for gl in range(2):
        arrived(kv.at[0, :, gl, c, x, 0:3], LINE + gl)
        here = kv.at[0, :, gl, c, x]
        for d in FAR_FIRST:
            send(here, here, xs[d - 1], BX + 3 * gl, BX + 3 * gl + d - 1)
        send(here, here, partner, CORE + gl)
    arrived(kv.at[1, yk, yg, c, x, 0:3], LINE + 2)
    for d in FAR_FIRST:
        here = kv.at[1, yk, yg, c, x, 0:2]
        send(here, here, ys[d - 1], AY)
        here = kv.at[1, yk, yg, c, x, 2:4]
        send(here, here, xs[d - 1], AX)

    def send_state(d):
        start = pl.multiple_of(step(resp, d, RESP) * CHANNELS + zh * LANES, LANES)
        send(state_h.at[0, :, pl.ds(start, LANES)], state_in.at[d - 1], resps(d), STATES)

    each(RESP, send_state)

    length = lengths[0]
    weight = advantages[0] * F32(TOKENS * lax.axis_size("ctx")) / length.astype(F32)
    position = ctx * TOKENS + lax.broadcasted_iota(jnp.int32, (TOKENS, 1), 0)
    token_weight = jnp.where(position < length, weight, F32(0.0))
    ones = jnp.ones((8, 2 * SIZE), BF16)

    def prepare(quad, carry):
        for i in range(2):
            pair = quad * 2 + i
            cols = pl.ds(pl.multiple_of(pair * 2 * SIZE, 2 * SIZE), 2 * SIZE)
            scaled = (grads[0, :, cols].astype(F32) * token_weight).astype(BF16)
            grads[0, :, cols] = scaled
            product = scaled.astype(F32) * outputs[0, :, cols].astype(F32)
            product = jnp.concatenate([product[:, 0:SIZE], product[:, SIZE:2 * SIZE]], axis=0)
            high = product.astype(BF16)
            low = (product - high.astype(F32)).astype(BF16)
            both = jnp.concatenate([high, low], axis=1)
            inners[pair] = lax.dot_general(ones, both, NT, preferred_element_type=F32)
        return carry

    for i in range(6, 9):
        loads[i].wait()
    own_t[...] = own[0] * LOG2E
    lax.fori_loop(0, 6, prepare, 0)

    arrived(tiles_in.at[0:7], TILES)
    span_all = jnp.ones((8, LANES), F32)
    carry_all = jnp.zeros((8, LANES), F32)
    for k in range(GROUP - 1, -1, -1):
        carry_all = tiles_in[k, 1] * carry_all + tiles_in[k, 0]
        span_all = span_all * tiles_in[k, 1]
    group_out[0] = carry_all
    group_out[1] = span_all
    for d in range(1, X):
        send(group_out, group_in.at[x], xs[d - 1], MAPS)
    group_in[x] = group_out[...]

    def second_gather():
        by_x = kv.at[1, :, :, c, x, 0:2]
        by_y = kv.at[1, yk, yg, c, :, 2:4]
        arrived(kv.at[1, 0, 0, c, 0:3, 0:2], AY)
        arrived(kv.at[1, 0, 0, c, 0:3, 2:4], AX)
        for d in FAR_FIRST:
            send(by_x, by_x, xs[d - 1], BX + 6, BX + 6 + d - 1)
            send(by_y, by_y, ys[d - 1], BY, BY + d - 1)
        send(by_x, by_x, partner, CORE + 2)
        send(by_y, by_y, partner, CORE + 2)

    def pass_head(gl):
        for d in FAR_LAST:
            here = kv.at[0, :, gl, c, step(x, -d, X)]
            arrived(here, BX + 3 * gl + d - 1)
            send(here, here, partner, CORE + gl)

    def pass_chunk():
        for d in FAR_LAST:
            here = kv.at[1, :, :, c, step(x, -d, X), 0:2]
            arrived(here, BX + 6 + d - 1)
            send(here, here, partner, CORE + 2)
            from_y = step(y, -d, Y)
            here = kv.at[1, lax.div(from_y, 2), lax.rem(from_y, 2), c, :, 2:4]
            arrived(here, BY + d - 1)
            send(here, here, partner, CORE + 2)

    def carry_back():
        for i in range(10, 13):
            loads[i].wait()
        arrived(state_in.at[0:15], STATES)
        arrived(group_in.at[0:3], MAPS)
        final = state_own[...].astype(F32) + jnp.sum(state_in[...].astype(F32), axis=0)
        incoming = jnp.where(c == 0, final[0:8], final[8:16])
        for k in range(X - 1, 0, -1):
            passed = group_in[k, 1] * incoming + group_in[k, 0]
            incoming = jnp.where(x < k, passed, incoming)
        for k in range(GROUP - 1, -1, -1):
            back_out[k] = incoming
            incoming = tiles_in[k, 1] * incoming + tiles_in[k, 0]
        each(GROUP, lambda d: send(back_out.at[step(q, d, GROUP)], back_in.at[q], group(d), BACKS))
        back_in[q] = back_out[q]

    def rows(ref, pair):
        heads = (2 * pair, 2 * pair + 1)
        return jnp.concatenate([ref[0, :, h * SIZE:(h + 1) * SIZE] for h in heads], axis=0)

    def keys_of(g):
        return kv[g // 2, 0, g % 2].reshape(KEYS, SIZE)

    def begin(pair):
        g = pair // 4
        values_g = kv[g // 2, 1, g % 2].reshape(KEYS, SIZE)
        scores = lax.dot_general(keys_of(g), rows(queries, pair), NT, preferred_element_type=F32) * (SCALE * LOG2E)
        dprobs = lax.dot_general(values_g, rows(grads, pair), NT, preferred_element_type=F32)
        return scores, dprobs

    def end(pair, begun, transposed, sums):
        scores, dprobs = begun
        h = 2 * pair
        inner = inners[pair, 0:1]
        own2 = jnp.concatenate([own_t[h:h + 1], own_t[h + 1:h + 2]], axis=1)
        top = jnp.maximum(jnp.max(scores, axis=0, keepdims=True), own2)
        powers = jnp.exp2(scores - top)
        total = jnp.sum(powers, axis=0, keepdims=True) + jnp.exp2(own2 - top)
        probs = powers * (1.0 / total)
        dscores = (probs * (dprobs - inner)).astype(BF16)
        query_t = jnp.dot(transposed, dscores, preferred_element_type=F32) * SCALE
        for i in range(2):
            part = query_t[:, i * SIZE:(i + 1) * SIZE].T.astype(BF16)
            query_out[0, :, (h + i) * SIZE:(h + i + 1) * SIZE] = part
        return (
            sums[0] + jnp.dot(dscores, rows(queries, pair), preferred_element_type=F32),
            sums[1] + jnp.dot(probs.astype(BF16), rows(grads, pair), preferred_element_type=F32),
        )

    def ship(g, sums):
        ch, gl = g // 2, g % 2
        for kind in range(2):
            partial[ch, kind, gl] = sums[kind].astype(BF16).reshape(partial.shape[3:])
        send(partial.at[ch, :, gl, other], core_in.at[ch, :, gl], partner, HALVES + g)
        store(g).start()

    def join(g):
        ch, gl = g // 2, g % 2
        arrived(core_in.at[ch, :, gl], HALVES + g)
        for kind in range(2):
            pairs[ch, kind * 2 + gl] = (
                partial[ch, kind, gl, c].astype(F32) + core_in[ch, kind, gl].astype(F32)
            ).astype(BF16)

    def first_hop(ch):
        for d in FAR_FIRST:
            send(pairs.at[ch, :, step(x, d, X), 0:2], first_in.at[ch, 0, d - 1], xs[d - 1], FIRST + 2 * ch)
            send(pairs.at[ch, step(y, d, Y), :, 2:4], first_in.at[ch, 1, d - 1], ys[d - 1], FIRST + 2 * ch + 1)

    def second_hop(ch):
        for axis in range(2):
            arrived(first_in.at[ch, axis], FIRST + 2 * ch + axis)
            held = pairs[ch, :, x, 0:2] if axis == 0 else pairs[ch, y, :, 2:4]
            total = held.astype(F32)
            for d in range(3):
                total = total + first_in[ch, axis, d].astype(F32)
            firsts[ch, axis] = total.astype(BF16)
            for d in FAR_FIRST:
                to = step(y, d, Y) if axis == 0 else step(x, d, X)
                target = (ys if axis == 0 else xs)[d - 1]
                send(firsts.at[ch, axis, to], second_in.at[ch, axis, d - 1], target, SECOND + 2 * ch + axis)

    def to_lines(ch):
        for axis in range(2):
            arrived(second_in.at[ch, axis], SECOND + 2 * ch + axis)
            total = firsts[ch, axis, y if axis == 0 else x].astype(F32)
            for d in range(3):
                total = total + second_in[ch, axis, d].astype(F32)
            lines[ch, 2 * axis:2 * axis + 2] = total.astype(BF16)
        for i in range(1, ZH):
            to = step(zh, i, ZH)
            send(lines.at[ch, to], line_in.at[z], (x * GROUP + to * CORES + c, (1 + ch) * Y + y), LINES + ch)

        @pl.when(zl != 1 + ch)
        def _():
            send(lines.at[ch, zh], line_in.at[z], (ctx, (1 + ch) * Y + y), LINES + ch)

    def sum_line(ch):
        @pl.when(zl == 1 + ch)
        def _():
            line_in[z] = lines[ch, zh]
            arrived(line_in.at[0:15], LINES + ch)
            summed = jnp.sum(line_in[...].astype(F32), axis=0).astype(BF16)
            piece[...] = summed
            each(RESP, lambda d: send(piece, pieces.at[ch * Y + y], resps(d), PIECES + ch))
            pieces[ch * Y + y] = summed

    loads[9].wait()
    pass_head(0)
    second_gather()
    lax.fori_loop(6, 8, prepare, 0)
    pass_head(1)
    carry_back()
    arrived(kv.at[0, :, 0, other], CORE)
    begun = begin(0)
    for pair in range(HEADS // 2):
        g = pair // 4
        if pair % 4 == 0:
            transposed = keys_of(g).T
            sums = (jnp.zeros((KEYS, SIZE), F32),) * 2
        if pair == 3:
            arrived(kv.at[0, :, 1, other], CORE + 1)
        if pair == 4:
            pass_chunk()
        if pair == 7:
            arrived(kv.at[1, :, :, other], CORE + 2)
        ahead = begin(pair + 1) if pair + 1 < HEADS // 2 else None
        sums = end(pair, begun, transposed, sums)
        begun = ahead
        if pair % 4 == 3:
            ship(g, sums)
            if g == 1:
                join(0)
            if g == 2:
                join(1)
                first_hop(0)
    join(2)
    second_hop(0)
    join(3)
    first_hop(1)
    to_lines(0)

    arrived(back_in.at[0:7], BACKS)
    square_in[...] = jnp.zeros_like(square_in)
    square_in[0:16, 0:16] = input_map[...]
    in_t = square_in[...].T
    taken = steps * mamba_in[...].astype(F32)
    carry = jnp.concatenate(
        [jnp.concatenate([back_in[kt * 2 + nh] for kt in range(4)], axis=1) for nh in range(2)], axis=0
    )
    lane = lax.broadcasted_iota(jnp.int32, (STATE, LANES), 1)
    db = jnp.zeros((STATE, LANES), F32)
    for t in range(BLOCK - 1, -1, -1):
        adjoint = out_t[0:STATE, t:t + 1] * dy[t:t + 1] + carry
        total = jnp.sum(in_t[0:STATE, t:t + 1] * adjoint, axis=0, keepdims=True)
        mamba_out[t:t + 1, :] = steps[t:t + 1] * total
        term = adjoint * taken[t:t + 1]
        term = (term[:, 0:128] + term[:, 128:256]) + (term[:, 256:384] + term[:, 384:512])
        db = jnp.where(lane == t, jnp.sum(term, axis=1, keepdims=True), db)
        carry = decays[t] * adjoint
    db_out[...] = db

    second_hop(1)
    each(RESP, lambda d: send(db_out, db_in.at[d - 1], resps(d), SUMS))
    to_lines(1)
    sum_line(0)
    sum_line(1)
    arrived(db_in.at[0:15], SUMS)
    square[0:STATE, :] = db_out[...] + jnp.sum(db_in[...], axis=0)
    map_out[...] = square[...].T[0:16, 0:16]

    for gl in range(2):
        left(kv.at[0, :, gl, c, x, 0:3], LINE + gl)
        left(kv.at[0, :, gl, c, 0:3], BX + 3 * gl)
        left(kv.at[0, :, gl, c], CORE + gl)
    left(kv.at[1, 0, 0, c, x, 0:3], LINE + 2)
    left(tiles_out.at[0:7], TILES)
    left(kv.at[1, 0, 0, c, 0:3, 0:2], AY)
    left(kv.at[1, 0, 0, c, 0:3, 2:4], AX)
    left(kv.at[1, :, :, c, 0:3, 0:2], BX + 6)
    left(kv.at[0, :, 0, c, 0:3], BY)
    left(kv.at[1, :, :, c], CORE + 2)
    left(state_in.at[0:15], STATES)
    left(group_in.at[0:3], MAPS)
    left(back_out.at[0:7], BACKS)
    for g in range(KV_HEADS):
        left(core_in.at[g // 2, :, g % 2], HALVES + g)
    for ch in range(2):
        for axis in range(2):
            left(first_in.at[ch, axis], FIRST + 2 * ch + axis)
            left(second_in.at[ch, axis], SECOND + 2 * ch + axis)
    left(db_in.at[0:15], SUMS)
    for ch in range(2):

        @pl.when(zl == 1 + ch)
        def _():
            left(line_in.at[0:3], LINES + ch)
            left(line_in.at[0:15], PIECES + ch)

        @pl.when(zl != 1 + ch)
        def _():
            left(line_in.at[0:4], LINES + ch)

    for g in range(KV_HEADS):
        store(g).wait()

    for ch in range(2):

        @pl.when(zl == 1 + ch)
        def _():
            arrived(pieces.at[0:3], PIECES + ch)

        @pl.when(zl != 1 + ch)
        def _():
            arrived(pieces.at[0:4], PIECES + ch)

        for gl in range(2):
            cols = slice((ch * 2 + gl) * LANES, (ch * 2 + gl + 1) * LANES)
            key_grad[:, cols] = pieces[ch * Y + gl].astype(F32) * SCALE
            value_grad[:, cols] = pieces[ch * Y + 2 + gl].astype(F32)


def finish_kernel(*refs):
    given, results, held = refs[0:5], refs[5:10], refs[10:15]
    sem_in, sem_out = refs[15], refs[16]
    part = (given[0].at[0], held[0].at[0], results[0].at[0])
    moves = []
    for i in range(8):
        rows = slice(i * BLOCK, (i + 1) * BLOCK)
        moves.append(tuple(ref.at[rows] for ref in part))
    moves += [(given[i], held[i], results[i]) for i in range(1, 5)]
    copies_in = [pltpu.make_async_copy(src, mid, sem_in.at[i]) for i, (src, mid, _) in enumerate(moves)]
    copies_out = [pltpu.make_async_copy(mid, dst, sem_out.at[i]) for i, (_, mid, dst) in enumerate(moves)]
    for copy in copies_in:
        copy.start()
    for first, then in zip(copies_in, copies_out):
        first.wait()
        then.start()
    for copy in copies_out:
        copy.wait()


def on_device(
    queries, attention_output, grad_out, own_log_sum_exp, prompt_keys, prompt_value_rows, advantages, lengths,
    mamba_in, step_size, decay_rate, input_map, output_map, mamba_grad, state_grad,
):
    smem = pl.BlockSpec(memory_space=pltpu.SMEM)
    anywhere = pl.BlockSpec(memory_space=pl.ANY)
    tile = (ZH, BLOCK, LANES)
    half = (2, BLOCK, LANES)
    wide = (1, TOKENS, HEADS * SIZE)
    block_grad = jax.ShapeDtypeStruct((BLOCK, KV_HEADS * SIZE), F32)
    results = (
        jax.ShapeDtypeStruct(wide, BF16),
        block_grad,
        block_grad,
        jax.ShapeDtypeStruct((BLOCK, CHANNELS), F32),
        jax.ShapeDtypeStruct((BLOCK, STATE), F32),
    )
    computed = pl.pallas_call(
        kernel,
        out_shape=results,
        in_specs=[smem] * 2 + [anywhere] * 13,
        out_specs=(anywhere,) + (VMEM,) * 4,
        scratch_shapes=[
            pltpu.VMEM(wide, BF16),
            pltpu.VMEM(wide, BF16),
            pltpu.VMEM(wide, BF16),
            pltpu.VMEM((1, HEADS, TOKENS), F32),
            pltpu.VMEM((BLOCK, KV_HEADS * SIZE), BF16),
            pltpu.VMEM((BLOCK, KV_HEADS * SIZE), BF16),
            pltpu.VMEM((BLOCK, CHANNELS), BF16),
            pltpu.VMEM((BLOCK, CHANNELS), F32),
            pltpu.VMEM((STATE, CHANNELS), F32),
            pltpu.VMEM((BLOCK, STATE), F32),
            pltpu.VMEM((BLOCK, STATE), F32),
            pltpu.VMEM((BLOCK, CHANNELS), BF16),
            pltpu.VMEM((STATE, LANES), BF16),
            pltpu.VMEM((2, 2, 2, BLOCK, LANES), BF16),
            pltpu.VMEM((2, 2, 2, CORES, X) + tile, BF16),
            pltpu.VMEM((HEADS, TOKENS), F32),
            pltpu.VMEM((HEADS // 2, 8, 2 * TOKENS), F32),
            pltpu.VMEM((LANES, LANES), F32),
            pltpu.VMEM((LANES, LANES), F32),
            pltpu.VMEM((BLOCK, STATE, CHANNELS), F32),
            pltpu.VMEM((GROUP, 2, 8, LANES), F32),
            pltpu.VMEM((GROUP, 2, 8, LANES), F32),
            pltpu.VMEM((RESP - 1, STATE, LANES), BF16),
            pltpu.VMEM((2, 8, LANES), F32),
            pltpu.VMEM((X, 2, 8, LANES), F32),
            pltpu.VMEM((GROUP, 8, LANES), F32),
            pltpu.VMEM((GROUP, 8, LANES), F32),
            pltpu.VMEM((STATE, LANES), F32),
            pltpu.VMEM((RESP - 1, STATE, LANES), F32),
            pltpu.VMEM((2, 2, 2, CORES, X) + tile, BF16),
            pltpu.VMEM((2, 2, 2, X) + tile, BF16),
            pltpu.VMEM((2, 4, X) + tile, BF16),
            pltpu.VMEM((2, 2, 3, 4) + half, BF16),
            pltpu.VMEM((2, 2, 4) + half, BF16),
            pltpu.VMEM((2, 2, 3) + half, BF16),
            pltpu.VMEM((2,) + tile, BF16),
            pltpu.VMEM((Z, BLOCK, LANES), BF16),
            pltpu.VMEM((BLOCK, LANES), BF16),
            pltpu.VMEM((2 * Y, BLOCK, LANES), BF16),
            pltpu.VMEM(wide, BF16),
            pltpu.SemaphoreType.DMA((13,)),
            pltpu.SemaphoreType.DMA((KV_HEADS,)),
            pltpu.SemaphoreType.DMA((SEMS,)),
            pltpu.SemaphoreType.DMA((SEMS,)),
        ],
        compiler_params=pltpu.CompilerParams(
            collective_id=0, has_side_effects=True, vmem_limit_bytes=56 * 2**20
        ),
        name="whole",
    )(
        advantages, lengths, queries, attention_output, grad_out, jnp.swapaxes(own_log_sum_exp, 1, 2), prompt_keys,
        prompt_value_rows, mamba_in, step_size, decay_rate, input_map, output_map, mamba_grad, state_grad,
    )
    return pl.pallas_call(
        finish_kernel,
        out_shape=results,
        in_specs=[anywhere] * 5,
        out_specs=(anywhere,) * 5,
        scratch_shapes=[pltpu.VMEM(r.shape, r.dtype) for r in results]
        + [pltpu.SemaphoreType.DMA((12,)), pltpu.SemaphoreType.DMA((12,))],
        compiler_params=pltpu.CompilerParams(vmem_limit_bytes=60 * 2**20),
        name="finish",
    )(*computed)


def solution(mesh):
    placed = (
        P("resp", "ctx", None),
        P("resp", "ctx", None),
        P("resp", "ctx", None),
        P("resp", "ctx", None),
        P("ctx", None),
        P("ctx", None),
        P("resp"),
        P("resp"),
        P("ctx", "resp"),
        P("ctx", "resp"),
        P(None, "resp"),
        P("ctx", None),
        P("ctx", None),
        P("ctx", "resp"),
        P("resp", None, None),
    )
    return jax.shard_map(
        on_device,
        mesh=mesh,
        in_specs=placed,
        out_specs=(
            P("resp", "ctx", None),
            P("ctx", None),
            P("ctx", None),
            P("ctx", "resp"),
            P("ctx", None),
        ),
        check_vma=False,
    )
```
